32 devices in a mesh: tile: 4 (over x, core), gz: 8 (over z, y).
Axes of the slice: x: 2, y: 2, z: 4, core: 2. Of those that a mesh axis runs over, the one named last changes fastest.
Arguments:
- planes: bfloat16 [32, 3, 512, 1024], P('gz', None, 'tile'), may hold values from -8 to 8
- level_gain: float32 [4], replicated, may hold values from 3 to 12
Outputs:
- joined: bfloat16 [3, 512, 1024], P(None, ('tile', 'gz'))
The draws below stay inside these ranges and needn't reach their ends.
All inputs are finite; a program needn't handle non-finite values.
Results may differ from the reference program's by a relative error of at most 0.0068.
The reference program's roundings to bfloat16 on the way (of `luminance`) count: a program that leaves them out, or rounds other values in their place, can miss the bound.
Values may be sent and summed in bfloat16 or wider, within the bound.
No kernel may reach another device: no remote copies, remote signals or barrier semaphores. Data moves between devices by JAX's collectives and lax.ppermute only.
A program may use at most 192 MiB of HBM per device.

```python
import math
import jax
import jax.numpy as jnp
from jax import lax

W = 1024
LEVELS = 4
Z = 32
H = 512


def draw_planes(key, part):
    keys = jax.random.split(key, 10)
    low = jnp.log(0.3)
    high = jnp.log(1.5)
    row_amp = jnp.exp(jax.random.uniform(keys[1], (Z, 1, H, 1), jnp.float32, low, high))
    col_amp = jnp.exp(jax.random.uniform(keys[2], (Z, 1, 1, W), jnp.float32, low, high))
    noise = jax.random.normal(keys[0], (Z, 3, H, W), jnp.float32)
    values = noise * row_amp * col_amp
    values = jnp.clip(values, -8.0, 8.0)
    block_rows = H // 16
    block_cols = W // 16
    chosen = jax.random.uniform(keys[4], (block_rows, block_cols), jnp.float32) < 0.12
    first_plane = jax.random.randint(keys[5], (block_rows, block_cols), 0, Z)
    second_plane = (first_plane + 1 + jax.random.randint(keys[6], (block_rows, block_cols), 0, Z - 1)) % Z
    strength = jax.random.uniform(keys[7], (block_rows, block_cols), jnp.float32, 5.0, 7.0)
    lowered = strength * (1.0 - jax.random.uniform(keys[8], (block_rows, block_cols), jnp.float32, 0.004, 0.008))
    offsets = jax.random.uniform(keys[9], (Z, 3, 1, 1), jnp.float32, -1.0, 1.0)
    plane_ids = jnp.arange(Z, dtype=jnp.int32)[:, None, None]
    is_first = (plane_ids == first_plane[None]) & chosen[None]
    is_second = (plane_ids == second_plane[None]) & chosen[None]
    amplitude = jnp.where(is_first, strength[None], jnp.where(is_second, lowered[None], 0.0))
    amplitude = jnp.repeat(jnp.repeat(amplitude, 16, axis=1), 16, axis=2)
    active = jnp.repeat(jnp.repeat(is_first | is_second, 16, axis=1), 16, axis=2)
    row_ids = jnp.arange(H, dtype=jnp.int32)[:, None]
    col_ids = jnp.arange(W, dtype=jnp.int32)[None, :]
    checker = jnp.where((row_ids + col_ids) % 2 == 0, 1.0, -1.0).astype(jnp.float32)
    pattern = amplitude[:, None] * checker[None, None] + offsets
    values = jnp.where(active[:, None], pattern, values)
    return jnp.clip(values, -8.0, 8.0).astype(jnp.bfloat16)


def setup_inputs(seed: int = 0) -> dict:
    key_of = jax.random.split(jax.random.key(seed), 3)
    planes = draw_planes(jax.random.fold_in(key_of[2], 71), 0)
    level_gain = jnp.clip(jnp.exp(jax.random.uniform(key_of[1], (LEVELS,), jnp.float32, math.log(3.0), math.log(12.0))), 3.0, 12.0)
    return {"planes": planes, "level_gain": level_gain}


TAPS = (0.0625, 0.25, 0.375, 0.25, 0.0625)


def smooth_rows(field, stride):
    count = field.shape[0]
    padded = jnp.pad(field, ((2 * stride, 2 * stride), (0, 0)))
    result = jnp.zeros_like(field)
    for place, factor in enumerate(TAPS):
        result = result + factor * padded[place * stride: place * stride + count]
    return result


def smooth_cols(field, stride):
    count = field.shape[1]
    padded = jnp.pad(field, ((0, 0), (2 * stride, 2 * stride)))
    result = jnp.zeros_like(field)
    for place, factor in enumerate(TAPS):
        result = result + factor * padded[:, place * stride: place * stride + count]
    return result


def plane_energy(plane, level_gain):
    luminance = (0.299 * plane[0].astype(jnp.float32) + 0.587 * plane[1].astype(jnp.float32)
                 + 0.114 * plane[2].astype(jnp.float32)).astype(jnp.bfloat16)
    approx = lax.optimization_barrier(luminance).astype(jnp.float32)
    energy = jnp.zeros(approx.shape, jnp.float32)
    for level in range(LEVELS):
        stride = 2 ** level
        smoother = smooth_cols(smooth_rows(approx, stride), stride)
        detail = approx - smoother
        energy = energy + level_gain[level] * detail * detail
        approx = smoother
    return energy


def reference(planes, level_gain):
    scores = lax.map(lambda plane: plane_energy(plane, level_gain), planes)
    highest = jnp.max(scores, axis=0)

    def accumulate(carry, item):
        total, colour = carry
        score, plane = item
        weight = jnp.exp(score - highest)
        return (total + weight, colour + weight[None] * plane.astype(jnp.float32)), None

    start = (jnp.zeros(highest.shape, jnp.float32), jnp.zeros((3,) + highest.shape, jnp.float32))
    (total, colour), _ = lax.scan(accumulate, start, (scores, planes))
    return (colour / total[None]).astype(jnp.bfloat16)
```

```python
import functools

import jax
import jax.numpy as jnp
import numpy as np
from jax import lax
from jax.experimental import pallas as pl
from jax.experimental.pallas import tpu as pltpu
from jax.sharding import PartitionSpec as P

LEVELS = 4
TAPS = (1, 4, 6, 4, 1)
HALO = 32
SIDE = 64
LANES = 128


def band_products(count):
    made = []
    whole = np.eye(count, dtype=np.int64)
    for level in range(LEVELS):
        step = np.zeros((count, count), np.int64)
        for place, tap in enumerate(TAPS):
            step += tap * np.eye(count, k=(place - 2) * 2**level, dtype=np.int64)
        whole = step @ whole
        made.append(whole)
    return made


def split_exact(matrix):
    high = matrix.astype(jnp.bfloat16).astype(np.int64)
    return high, matrix - high


def row_matrices(image_rows, rows):
    bands = band_products(image_rows)
    tiles = []
    for tile in range(image_rows // rows):
        parts = []
        for level, band in enumerate(bands):
            window = np.pad(band, ((0, 0), (HALO, HALO)))
            window = window[tile * rows : (tile + 1) * rows, tile * rows : (tile + 1) * rows + 2 * HALO]
            high, low = split_exact(window)
            scale = 1.0 / 16 ** (level + 1)
            parts.append(high * scale)
            if level >= 2:
                parts.append(low * scale)
        tiles.append(np.concatenate(parts, axis=0))
    return np.stack(tiles).astype(jnp.bfloat16)


def column_matrices(columns):
    bands = band_products(columns)
    blocks = columns // LANES
    cases = []
    for block in (0, 1, blocks - 1):
        parts = []
        for level, band in enumerate(bands):
            window = np.pad(band.T, ((SIDE, SIDE), (0, 0)))
            window = window[block * LANES : block * LANES + LANES + 2 * SIDE, block * LANES : (block + 1) * LANES]
            high, low = split_exact(window)
            scale = 1.0 / 16 ** (level + 1)
            parts.append(high * scale)
            if level >= 2:
                parts.append(low * scale)
        cases.append(np.concatenate(parts, axis=1))
    return np.stack(cases).astype(jnp.bfloat16)


def dot(left, right):
    return jnp.dot(left, right, preferred_element_type=jnp.float32)


def luminance_of(colours):
    red, green, blue = (colours[channel].astype(jnp.float32) for channel in range(3))
    return (0.299 * red + 0.587 * green + 0.114 * blue).astype(jnp.bfloat16)


def state_kernel(tile_ref, gain_ref, planes_ref, above_ref, below_ref, row_ref, col_ref, out_ref, lum, wide, high, low):
    depth, _, rows, columns = planes_ref.shape
    blocks = columns // LANES
    padding = jnp.zeros((rows + 2 * HALO, LANES), jnp.float32)
    for plane in range(depth):
        own = luminance_of([planes_ref[plane, channel] for channel in range(3)])
        lum[plane] = own
        field = jnp.concatenate([above_ref[plane], own, below_ref[plane]], axis=0).astype(jnp.float32)
        field = jnp.concatenate([field, padding], axis=1)
        wide[plane] = pltpu.roll(field, SIDE, 1).astype(jnp.bfloat16)

    def rows_step(block, _):
        at = pl.ds(pl.multiple_of(block * LANES, LANES), LANES)
        for plane in range(depth):
            window = wide[plane, :, at]
            smooth = dot(row_ref[0], window)
            part = [smooth[k * rows : (k + 1) * rows] for k in range(6)]
            for level, value in enumerate((part[0], part[1], part[2] + part[3], part[4] + part[5])):
                top = value.astype(jnp.bfloat16)
                here = pl.ds(plane * rows, rows)
                high[level, here, at] = top
                low[level, here, at] = (value - top.astype(jnp.float32)).astype(jnp.bfloat16)
        return 0

    lax.fori_loop(0, blocks + 1, rows_step, 0)

    def columns_step(block, _):
        at = pl.ds(pl.multiple_of(block * LANES, LANES), LANES)
        window = pl.ds(pl.multiple_of(block * LANES, LANES), 2 * LANES)
        case = jnp.where(block == 0, 0, jnp.where(block == blocks - 1, 2, 1))
        approx = [lum[:, :, at].astype(jnp.float32).reshape(depth * rows, LANES)]
        for level in range(LEVELS):
            top, rest = high[level, :, window], low[level, :, window]
            if level < 2:
                taps = col_ref[case, :, level * LANES : (level + 1) * LANES]
                approx.append(dot(top, taps) + dot(rest, taps))
            else:
                first = (2 * level - 2) * LANES
                both = dot(top, col_ref[case, :, first : first + 2 * LANES])
                extra = dot(rest, col_ref[case, :, first : first + LANES])
                approx.append(both[:, :LANES] + both[:, LANES:] + extra)
        score = jnp.zeros((depth * rows, LANES), jnp.float32)
        for level in range(LEVELS):
            detail = approx[level] - approx[level + 1]
            score = score + gain_ref[level] * detail * detail
        score = score.reshape(depth, rows, LANES)
        peak = jnp.max(score, axis=0).astype(jnp.bfloat16)
        weight = jnp.exp(score - peak.astype(jnp.float32)[None])
        total = jnp.sum(weight, axis=0)
        inverse = 1.0 / total
        out_ref[0, :, at] = peak
        out_ref[1, :, at] = total.astype(jnp.bfloat16)
        for channel in range(3):
            colour = jnp.sum(weight * planes_ref[:, channel, :, at].astype(jnp.float32), axis=0)
            out_ref[2 + channel, :, at] = (colour * inverse).astype(jnp.bfloat16)
        return 0

    lax.fori_loop(0, blocks, columns_step, 0)


def local_state(planes, above, below, level_gain, tile_count):
    depth, _, rows, columns = planes.shape
    row_bands = jnp.asarray(row_matrices(rows * tile_count, rows))
    col_bands = jnp.asarray(column_matrices(columns))
    tile = lax.axis_index("tile").astype(jnp.int32).reshape(1)
    vmem = pl.BlockSpec(memory_space=pltpu.VMEM)
    wide = columns + LANES

    def whole(shape):
        return pl.BlockSpec(shape, lambda i, t: (0,) * len(shape))

    return pl.pallas_call(
        state_kernel,
        out_shape=jax.ShapeDtypeStruct((5, rows, columns), jnp.bfloat16),
        grid_spec=pltpu.PrefetchScalarGridSpec(
            num_scalar_prefetch=1,
            grid=(1,),
            in_specs=[
                pl.BlockSpec(memory_space=pltpu.SMEM),
                whole(planes.shape),
                whole(above.shape),
                whole(below.shape),
                pl.BlockSpec((1,) + row_bands.shape[1:], lambda i, t: (t[0], 0, 0)),
                whole(col_bands.shape),
            ],
            out_specs=whole((5, rows, columns)),
            scratch_shapes=[
                pltpu.VMEM((depth, rows, columns), jnp.bfloat16),
                pltpu.VMEM((depth, rows + 2 * HALO, wide), jnp.bfloat16),
                pltpu.VMEM((LEVELS, depth * rows, wide), jnp.bfloat16),
                pltpu.VMEM((LEVELS, depth * rows, wide), jnp.bfloat16),
            ],
        ),
        compiler_params=pltpu.CompilerParams(vmem_limit_bytes=56 * 2**20),
        name="local_state",
    )(tile, level_gain, planes, above, below, row_bands, col_bands)


def merge_kernel(*refs):
    *states, out_ref = refs
    peak = functools.reduce(jnp.maximum, [state[0].astype(jnp.float32) for state in states])
    total = jnp.zeros(peak.shape, jnp.float32)
    colour = [jnp.zeros(peak.shape, jnp.float32) for _ in range(3)]
    for state in states:
        weight = state[1].astype(jnp.float32) * jnp.exp(state[0].astype(jnp.float32) - peak)
        total = total + weight
        for channel in range(3):
            colour[channel] = colour[channel] + weight * state[2 + channel].astype(jnp.float32)
    for channel in range(3):
        out_ref[channel] = (colour[channel] / total).astype(jnp.bfloat16)


def merge(states):
    _, share, columns = states[0].shape
    return pl.pallas_call(
        merge_kernel,
        out_shape=jax.ShapeDtypeStruct((3, share, columns), jnp.bfloat16),
        compiler_params=pltpu.CompilerParams(vmem_limit_bytes=32 * 2**20),
        name="merge",
    )(*states)


def per_device(planes, level_gain):
    rows = planes.shape[2]
    tiles = lax.axis_size("tile")
    groups = lax.axis_size("gz")
    share = rows // groups
    head = luminance_of([planes[:, channel, :HALO] for channel in range(3)])
    tail = luminance_of([planes[:, channel, rows - HALO :] for channel in range(3)])
    above = lax.ppermute(tail, "tile", [(i, i + 1) for i in range(tiles - 1)])
    below = lax.ppermute(head, "tile", [(i + 1, i) for i in range(tiles - 1)])
    state = local_state(planes, above, below, level_gain, tiles)
    me = lax.axis_index("gz")
    states = [lax.dynamic_slice_in_dim(state, me * share, share, 1)]
    for other in range(1, groups):
        band = lax.dynamic_slice_in_dim(state, (me ^ other) * share, share, 1)
        states.append(lax.ppermute(band, "gz", [(i, i ^ other) for i in range(groups)]))
    return merge(states)


def solution(mesh):
    return jax.shard_map(
        per_device,
        mesh=mesh,
        in_specs=(P("gz", None, "tile", None), P()),
        out_specs=P(None, ("tile", "gz"), None),
        check_vma=False,
    )
```

```python
import functools

import jax
import jax.numpy as jnp
import numpy as np
from jax import lax
from jax.experimental import pallas as pl
from jax.experimental.pallas import tpu as pltpu
from jax.sharding import PartitionSpec as P

LEVELS = 4
TAPS = (1, 4, 6, 4, 1)
HALO = 32
SIDE = 64
LANES = 128


def band_products(count):
    made = []
    whole = np.eye(count)
    for level in range(LEVELS):
        step = sum(tap * np.eye(count, k=(place - 2) * 2**level) for place, tap in enumerate(TAPS))
        whole = step @ whole
        made.append(whole)
    return made


def split_exact(matrix):
    high = matrix.astype(jnp.bfloat16).astype(matrix.dtype)
    return high, matrix - high


def row_matrices(image_rows, rows):
    bands = band_products(image_rows)
    tiles = []
    for tile in (0, 1, image_rows // rows - 1):
        parts = []
        for level, band in enumerate(bands):
            window = np.pad(band, ((0, 0), (HALO, HALO)))
            window = window[tile * rows : (tile + 1) * rows, tile * rows : (tile + 1) * rows + 2 * HALO]
            high, low = split_exact(window)
            scale = 1.0 / 16 ** (level + 1)
            parts.append(high * scale)
            if level >= 2:
                parts.append(low * scale)
        tiles.append(np.concatenate(parts, axis=0))
    return np.stack(tiles).astype(jnp.bfloat16)


def column_matrices(columns):
    bands = band_products(columns)
    blocks = columns // LANES
    cases = []
    for block in (0, 1, blocks - 1):
        parts = []
        for level, band in enumerate(bands):
            window = np.pad(band.T, ((SIDE, SIDE), (0, 0)))
            window = window[block * LANES : block * LANES + LANES + 2 * SIDE, block * LANES : (block + 1) * LANES]
            high, low = split_exact(window)
            scale = 1.0 / 16 ** (level + 1)
            parts.append(high * scale)
            if level >= 2:
                parts.append(low * scale)
        cases.append(np.concatenate(parts, axis=1))
    return np.stack(cases).astype(jnp.bfloat16)


def dot(left, right):
    return jnp.dot(left, right, preferred_element_type=jnp.float32)


def luminance_of(colours):
    red, green, blue = (colours[channel].astype(jnp.float32) for channel in range(3))
    return (0.299 * red + 0.587 * green + 0.114 * blue).astype(jnp.bfloat16)


def combine(states):
    states = [[part.astype(jnp.float32) for part in state] for state in states]
    peak = functools.reduce(jnp.maximum, [state[0] for state in states])
    weights = [state[1] * jnp.exp(state[0] - peak) for state in states]
    total = sum(weights[1:], weights[0])
    inverse = 1.0 / total
    colours = []
    for channel in range(2, 5):
        terms = [weight * state[channel] for weight, state in zip(weights, states)]
        colours.append(sum(terms[1:], terms[0]) * inverse)
    return [peak, total] + colours


def state_kernel(slow, gain_ref, planes_ref, above_ref, below_ref, row_ref, col_ref, *refs):
    *outs, lum, wide, high, low, held = refs
    depth, _, rows, columns = planes_ref.shape
    groups, _, share, _ = held.shape
    fast = groups // slow
    split = outs[0].shape[-1]
    blocks = columns // LANES
    tile, tiles = lax.axis_index("tile"), lax.axis_size("tile")
    tile_case = jnp.where(tile == 0, 0, jnp.where(tile == tiles - 1, 2, 1))
    padding = jnp.zeros((rows + 2 * HALO, LANES), jnp.float32)
    for plane in range(depth):
        own = luminance_of([planes_ref[plane, channel] for channel in range(3)])
        lum[plane] = own
        field = jnp.concatenate([above_ref[plane], own, below_ref[plane]], axis=0).astype(jnp.float32)
        field = jnp.concatenate([field, padding], axis=1)
        wide[plane] = pltpu.roll(field, SIDE, 1).astype(jnp.bfloat16)

    for start in range(0, columns + LANES, 2 * LANES):
        at = pl.ds(start, min(2 * LANES, columns + LANES - start))
        for plane in range(depth):
            here = pl.ds(plane * rows, rows)
            smooth = dot(row_ref[tile_case], wide[plane, :, at])
            part = [smooth[k * rows : (k + 1) * rows] for k in range(6)]
            for level, value in enumerate((part[0], part[1], part[2] + part[3], part[4] + part[5])):
                top = value.astype(jnp.bfloat16)
                high[level, here, at] = top
                low[level, here, at] = (value - top.astype(jnp.float32)).astype(jnp.bfloat16)

    for block in range(blocks):
        at = pl.ds(block * LANES, LANES)
        window = pl.ds(block * LANES, 2 * LANES)
        case = 0 if block == 0 else 2 if block == blocks - 1 else 1
        approx = [lum[:, :, at].astype(jnp.float32).reshape(depth * rows, LANES)]
        for level in range(LEVELS):
            top, rest = high[level, :, window], low[level, :, window]
            if level < 2:
                taps = col_ref[case, :, level * LANES : (level + 1) * LANES]
                approx.append(dot(top, taps) + dot(rest, taps))
            else:
                first = (2 * level - 2) * LANES
                both = dot(top, col_ref[case, :, first : first + 2 * LANES])
                extra = dot(rest, col_ref[case, :, first : first + LANES])
                approx.append(both[:, :LANES] + both[:, LANES:] + extra)
        score = jnp.zeros((depth * rows, LANES), jnp.float32)
        for level in range(LEVELS):
            detail = approx[level] - approx[level + 1]
            score = score + gain_ref[level] * detail * detail
        score = score.reshape(depth, rows, LANES)
        peak = jnp.max(score, axis=0).astype(jnp.bfloat16)
        weight = jnp.exp(score - peak.astype(jnp.float32)[None])
        total = jnp.sum(weight, axis=0)
        inverse = 1.0 / total
        state = [peak, total.astype(jnp.bfloat16)]
        for channel in range(3):
            colour = jnp.sum(weight * planes_ref[:, channel, :, at].astype(jnp.float32), axis=0)
            state.append((colour * inverse).astype(jnp.bfloat16))
        for k, part in enumerate(state):
            held[:, k, :, at] = part.reshape(groups, share, LANES)

    group = lax.axis_index("gz")
    mine_slow, mine_fast = group // fast, group % fast
    for other in range(fast):
        for place in range(slow):
            outs[other][place] = held[place * fast + (mine_fast ^ other), :, :, :split]
    for other in range(slow):
        for place in range(fast):
            outs[fast + other][place] = held[(mine_slow ^ other) * fast + place, :, :, split:]


def local_state(planes, above, below, level_gain, slow, groups, tiles, split):
    depth, _, rows, columns = planes.shape
    fast, share = groups // slow, rows // groups
    row_bands = jnp.asarray(row_matrices(rows * tiles, rows))
    col_bands = jnp.asarray(column_matrices(columns))
    vmem = pl.BlockSpec(memory_space=pltpu.VMEM)
    wide = columns + LANES
    shapes = [(slow, 5, share, split)] * fast + [(fast, 5, share, columns - split)] * slow
    return pl.pallas_call(
        functools.partial(state_kernel, slow),
        out_shape=[jax.ShapeDtypeStruct(shape, jnp.bfloat16) for shape in shapes],
        in_specs=[pl.BlockSpec(memory_space=pltpu.SMEM)] + [vmem] * 5,
        out_specs=[vmem] * len(shapes),
        scratch_shapes=[
            pltpu.VMEM((depth, rows, columns), jnp.bfloat16),
            pltpu.VMEM((depth, rows + 2 * HALO, wide), jnp.bfloat16),
            pltpu.VMEM((LEVELS, depth * rows, wide), jnp.bfloat16),
            pltpu.VMEM((LEVELS, depth * rows, wide), jnp.bfloat16),
            pltpu.VMEM((groups, 5, share, columns), jnp.bfloat16),
        ],
        compiler_params=pltpu.CompilerParams(vmem_limit_bytes=40 * 2**20),
        name="local_state",
    )(level_gain, planes, above, below, row_bands, col_bands)


def merge_kernel(count, pick, *refs):
    states, outs, held = refs[:count], refs[count:-1], refs[-1]
    for place in range(held.shape[0]):
        for k, part in enumerate(combine([[state[place, k] for k in range(5)] for state in states])):
            held[place, k] = part.astype(jnp.bfloat16)
    place = pick(lax.axis_index("gz"))
    for other, out in enumerate(outs):
        out[...] = held[place ^ other]


def merge(states, pick):
    bands, _, share, columns = states[0].shape
    return pl.pallas_call(
        functools.partial(merge_kernel, len(states), pick),
        out_shape=[jax.ShapeDtypeStruct((5, share, columns), jnp.bfloat16)] * bands,
        scratch_shapes=[pltpu.VMEM(states[0].shape, jnp.bfloat16)],
        compiler_params=pltpu.CompilerParams(vmem_limit_bytes=16 * 2**20),
        name="merge",
    )(*states)


def join_kernel(counts, *refs):
    *refs, out_ref = refs
    start = 0
    for count in counts:
        states, refs = refs[:count], refs[count:]
        width = states[0].shape[-1]
        merged = combine([[state[k] for k in range(5)] for state in states])
        for channel in range(3):
            out_ref[channel, :, start : start + width] = merged[2 + channel].astype(jnp.bfloat16)
        start += width


def join(*parts):
    share = parts[0][0].shape[1]
    columns = sum(part[0].shape[2] for part in parts)
    return pl.pallas_call(
        functools.partial(join_kernel, [len(part) for part in parts]),
        out_shape=jax.ShapeDtypeStruct((3, share, columns), jnp.bfloat16),
        compiler_params=pltpu.CompilerParams(vmem_limit_bytes=16 * 2**20),
        name="join",
    )(*[state for part in parts for state in part])


def swap(states, groups, step):
    moved = [
        lax.ppermute(state, "gz", [(i, i ^ (k * step)) for i in range(groups)]) for k, state in enumerate(states) if k
    ]
    return [states[0]] + moved


def per_device(planes, level_gain):
    rows, columns = planes.shape[2:]
    tiles = lax.axis_size("tile")
    groups = lax.axis_size("gz")
    slow = min(4, groups)
    fast = groups // slow
    split = 5 * columns // 8
    head = luminance_of([planes[:, channel, :HALO] for channel in range(3)])
    tail = luminance_of([planes[:, channel, rows - HALO :] for channel in range(3)])
    above = lax.ppermute(tail, "tile", [(i, i + 1) for i in range(tiles - 1)])
    below = lax.ppermute(head, "tile", [(i + 1, i) for i in range(tiles - 1)])
    states = local_state(planes, above, below, level_gain, slow, groups, tiles, split)
    first = swap(states[:fast], groups, 1)
    second = swap(states[fast:], groups, fast)
    first = swap(merge(first, lambda group: group // fast), groups, fast)
    second = swap(merge(second, lambda group: group % fast), groups, 1)
    return join(first, second)


def solution(mesh):
    return jax.shard_map(
        per_device,
        mesh=mesh,
        in_specs=(P("gz", None, "tile", None), P()),
        out_specs=P(None, ("tile", "gz"), None),
        check_vma=False,
    )
```

```python
import functools

import jax
import jax.numpy as jnp
import numpy as np
from jax import lax
from jax.experimental import pallas as pl
from jax.experimental.pallas import tpu as pltpu
from jax.sharding import PartitionSpec as P

LEVELS = 4
TAPS = (1, 4, 6, 4, 1)
HALO = 32
SIDE = 64
LANES = 128


def band_products(count):
    made = []
    whole = np.eye(count)
    for level in range(LEVELS):
        step = sum(tap * np.eye(count, k=(place - 2) * 2**level) for place, tap in enumerate(TAPS))
        whole = step @ whole
        made.append(whole)
    return made


def split_exact(matrix):
    high = matrix.astype(jnp.bfloat16).astype(matrix.dtype)
    return high, matrix - high


def row_matrices(image_rows, rows):
    bands = band_products(image_rows)
    tiles = []
    for tile in (0, 1, image_rows // rows - 1):
        parts = []
        for level, band in enumerate(bands):
            window = np.pad(band, ((0, 0), (HALO, HALO)))
            window = window[tile * rows : (tile + 1) * rows, tile * rows : (tile + 1) * rows + 2 * HALO]
            high, low = split_exact(window)
            scale = 1.0 / 16 ** (level + 1)
            parts.append(high * scale)
            if level >= 2:
                parts.append(low * scale)
        tiles.append(np.concatenate(parts, axis=0))
    return np.stack(tiles).astype(jnp.bfloat16)


def column_matrices(columns):
    bands = band_products(columns)
    blocks = columns // LANES
    cases = []
    for block in (0, 1, blocks - 1):
        parts = []
        for level, band in enumerate(bands):
            window = np.pad(band.T, ((SIDE, SIDE), (0, 0)))
            window = window[block * LANES : block * LANES + LANES + 2 * SIDE, block * LANES : (block + 1) * LANES]
            high, low = split_exact(window)
            scale = 1.0 / 16 ** (level + 1)
            parts.append(high * scale)
            if level >= 2:
                parts.append(low * scale)
        cases.append(np.concatenate(parts, axis=1))
    return np.stack(cases).astype(jnp.bfloat16)


def dot(left, right):
    return jnp.dot(left, right, preferred_element_type=jnp.float32)


def luminance_of(colours):
    red, green, blue = (colours[channel].astype(jnp.float32) for channel in range(3))
    return (0.299 * red + 0.587 * green + 0.114 * blue).astype(jnp.bfloat16)


def combine(states):
    states = [[part.astype(jnp.float32) for part in state] for state in states]
    peak = functools.reduce(jnp.maximum, [state[0] for state in states])
    weights = [state[1] * jnp.exp(state[0] - peak) for state in states]
    total = sum(weights[1:], weights[0])
    inverse = 1.0 / total
    colours = []
    for channel in range(2, 5):
        terms = [weight * state[channel] for weight, state in zip(weights, states)]
        colours.append(sum(terms[1:], terms[0]) * inverse)
    return [peak, total] + colours


def edge_kernel(planes_ref, core_ref, far_ref, edges, arrived):
    rows = planes_ref.shape[2]
    odd = lax.axis_index("tile") % 2
    tail, head = rows - HALO, 0
    copies = []
    for side, start in enumerate((jnp.where(odd == 0, tail, head), jnp.where(odd == 0, head, tail))):
        at = pl.ds(pl.multiple_of(start, HALO), HALO)
        copies.append(pltpu.make_async_copy(planes_ref.at[:, :, at], edges.at[side], arrived.at[side]))
        copies[-1].start()
    for side, out in enumerate((core_ref, far_ref)):
        copies[side].wait()
        for plane in range(planes_ref.shape[0]):
            out[plane] = luminance_of([edges[side, plane, channel] for channel in range(3)])


def edge_luminance(planes):
    depth, channels, rows, columns = planes.shape
    vmem = pl.BlockSpec(memory_space=pltpu.VMEM)
    return pl.pallas_call(
        edge_kernel,
        out_shape=[jax.ShapeDtypeStruct((depth, HALO, columns), jnp.bfloat16)] * 2,
        in_specs=[pl.BlockSpec(memory_space=pl.ANY)],
        out_specs=[vmem] * 2,
        scratch_shapes=[
            pltpu.VMEM((2, depth, channels, HALO, columns), jnp.bfloat16),
            pltpu.SemaphoreType.DMA((2,)),
        ],
        compiler_params=pltpu.CompilerParams(vmem_limit_bytes=52 * 2**20),
        name="edge_luminance",
    )(planes)


def own_kernel(planes_ref, rows_ref, cols_ref, stack_ref, lum_ref, wide_ref, row_ref, col_ref, arrived):
    depth, _, rows, columns = planes_ref.shape
    tile, tiles = lax.axis_index("tile"), lax.axis_size("tile")
    tile_case = jnp.where(tile == 0, 0, jnp.where(tile == tiles - 1, 2, 1))
    copies = [pltpu.make_async_copy(planes_ref.at[p], stack_ref.at[p], arrived.at[p]) for p in range(depth)]
    copies.append(pltpu.make_async_copy(rows_ref.at[tile_case], row_ref, arrived.at[depth]))
    copies.append(pltpu.make_async_copy(cols_ref, col_ref, arrived.at[depth + 1]))
    for copy in copies:
        copy.start()
    padding = jnp.zeros((rows, LANES), jnp.float32)
    for plane in range(depth):
        copies[plane].wait()
        own = luminance_of([stack_ref[plane, channel] for channel in range(3)])
        lum_ref[plane] = own
        field = jnp.concatenate([own.astype(jnp.float32), padding], axis=1)
        wide_ref[plane] = pltpu.roll(field, SIDE, 1).astype(jnp.bfloat16)
    for copy in copies[depth:]:
        copy.wait()


def own_rows(planes, tiles):
    depth, channels, rows, columns = planes.shape
    row_bands = jnp.asarray(row_matrices(rows * tiles, rows))
    col_bands = jnp.asarray(column_matrices(columns))
    vmem = pl.BlockSpec(memory_space=pltpu.VMEM)
    shapes = [planes.shape, (depth, rows, columns), (depth, rows, columns + LANES), row_bands.shape[1:], col_bands.shape]
    return pl.pallas_call(
        own_kernel,
        out_shape=[jax.ShapeDtypeStruct(shape, jnp.bfloat16) for shape in shapes],
        in_specs=[pl.BlockSpec(memory_space=pl.ANY)] * 3,
        out_specs=[vmem] * len(shapes),
        scratch_shapes=[pltpu.SemaphoreType.DMA((depth + 2,))],
        compiler_params=pltpu.CompilerParams(vmem_limit_bytes=44 * 2**20),
        cost_estimate=pl.CostEstimate(flops=2**24, bytes_accessed=10 * 2**20, transcendentals=0),
        name="own_rows",
    )(planes, row_bands, col_bands)


def state_kernel(slow, gain_ref, planes_ref, lum_ref, wide_ref, core_ref, far_ref, row_ref, col_ref, *refs):
    *outs, halo, high, low, held = refs
    depth, _, rows, columns = planes_ref.shape
    groups, _, share, _ = held.shape
    fast = groups // slow
    split = outs[0].shape[-1]
    blocks = columns // LANES
    odd = lax.axis_index("tile") % 2
    padding = jnp.zeros((HALO, LANES), jnp.float32)

    def place_halo(above_ref, below_ref):
        for side, ref in enumerate((above_ref, below_ref)):
            for plane in range(depth):
                field = jnp.concatenate([ref[plane].astype(jnp.float32), padding], axis=1)
                halo[side, plane] = pltpu.roll(field, SIDE, 1).astype(jnp.bfloat16)

    pl.when(odd == 0)(lambda: place_halo(far_ref, core_ref))
    pl.when(odd == 1)(lambda: place_halo(core_ref, far_ref))

    for start in range(0, columns + LANES, 2 * LANES):
        at = pl.ds(start, min(2 * LANES, columns + LANES - start))
        for plane in range(depth):
            here = pl.ds(plane * rows, rows)
            window = jnp.concatenate([halo[0, plane, :, at], wide_ref[plane, :, at], halo[1, plane, :, at]], axis=0)
            smooth = dot(row_ref[...], window)
            part = [smooth[k * rows : (k + 1) * rows] for k in range(6)]
            for level, value in enumerate((part[0], part[1], part[2] + part[3], part[4] + part[5])):
                top = value.astype(jnp.bfloat16)
                high[level, here, at] = top
                low[level, here, at] = (value - top.astype(jnp.float32)).astype(jnp.bfloat16)

    for block in range(blocks):
        at = pl.ds(block * LANES, LANES)
        window = pl.ds(block * LANES, 2 * LANES)
        case = 0 if block == 0 else 2 if block == blocks - 1 else 1
        approx = [lum_ref[:, :, at].astype(jnp.float32).reshape(depth * rows, LANES)]
        for level in range(LEVELS):
            top, rest = high[level, :, window], low[level, :, window]
            if level < 2:
                taps = col_ref[case, :, level * LANES : (level + 1) * LANES]
                approx.append(dot(top, taps) + dot(rest, taps))
            else:
                first = (2 * level - 2) * LANES
                both = dot(top, col_ref[case, :, first : first + 2 * LANES])
                extra = dot(rest, col_ref[case, :, first : first + LANES])
                approx.append(both[:, :LANES] + both[:, LANES:] + extra)
        score = jnp.zeros((depth * rows, LANES), jnp.float32)
        for level in range(LEVELS):
            detail = approx[level] - approx[level + 1]
            score = score + gain_ref[level] * detail * detail
        score = score.reshape(depth, rows, LANES)
        peak = jnp.max(score, axis=0).astype(jnp.bfloat16)
        weight = jnp.exp(score - peak.astype(jnp.float32)[None])
        total = jnp.sum(weight, axis=0)
        inverse = 1.0 / total
        state = [peak, total.astype(jnp.bfloat16)]
        for channel in range(3):
            colour = jnp.sum(weight * planes_ref[:, channel, :, at].astype(jnp.float32), axis=0)
            state.append((colour * inverse).astype(jnp.bfloat16))
        for k, part in enumerate(state):
            held[:, k, :, at] = part.reshape(groups, share, LANES)

    group = lax.axis_index("gz")
    mine_slow, mine_fast = group // fast, group % fast
    for other in range(fast):
        for place in range(slow):
            outs[other][place] = held[place * fast + (mine_fast ^ other), :, :, :split]
    for other in range(slow):
        for place in range(fast):
            outs[fast + other][place] = held[(mine_slow ^ other) * fast + place, :, :, split:]


def local_state(own, core, far, level_gain, slow, groups, split):
    depth, _, rows, columns = own[0].shape
    fast, share = groups // slow, rows // groups
    vmem = pl.BlockSpec(memory_space=pltpu.VMEM)
    wide = columns + LANES
    shapes = [(slow, 5, share, split)] * fast + [(fast, 5, share, columns - split)] * slow
    return pl.pallas_call(
        functools.partial(state_kernel, slow),
        out_shape=[jax.ShapeDtypeStruct(shape, jnp.bfloat16) for shape in shapes],
        in_specs=[pl.BlockSpec(memory_space=pltpu.SMEM)] + [vmem] * 7,
        out_specs=[vmem] * len(shapes),
        scratch_shapes=[
            pltpu.VMEM((2, depth, HALO, wide), jnp.bfloat16),
            pltpu.VMEM((LEVELS, depth * rows, wide), jnp.bfloat16),
            pltpu.VMEM((LEVELS, depth * rows, wide), jnp.bfloat16),
            pltpu.VMEM((groups, 5, share, columns), jnp.bfloat16),
        ],
        compiler_params=pltpu.CompilerParams(vmem_limit_bytes=40 * 2**20),
        name="local_state",
    )(level_gain, *own[:3], core, far, *own[3:])


def merge_kernel(count, pick, *refs):
    states, outs, held = refs[:count], refs[count:-1], refs[-1]
    for place in range(held.shape[0]):
        for k, part in enumerate(combine([[state[place, k] for k in range(5)] for state in states])):
            held[place, k] = part.astype(jnp.bfloat16)
    place = pick(lax.axis_index("gz"))
    for other, out in enumerate(outs):
        out[...] = held[place ^ other]


def merge(states, pick):
    bands, _, share, columns = states[0].shape
    return pl.pallas_call(
        functools.partial(merge_kernel, len(states), pick),
        out_shape=[jax.ShapeDtypeStruct((5, share, columns), jnp.bfloat16)] * bands,
        scratch_shapes=[pltpu.VMEM(states[0].shape, jnp.bfloat16)],
        compiler_params=pltpu.CompilerParams(vmem_limit_bytes=16 * 2**20),
        name="merge",
    )(*states)


def join_kernel(counts, *refs):
    *refs, out_ref = refs
    start = 0
    for count in counts:
        states, refs = refs[:count], refs[count:]
        width = states[0].shape[-1]
        merged = combine([[state[k] for k in range(5)] for state in states])
        for channel in range(3):
            out_ref[channel, :, start : start + width] = merged[2 + channel].astype(jnp.bfloat16)
        start += width


def join(*parts):
    share = parts[0][0].shape[1]
    columns = sum(part[0].shape[2] for part in parts)
    return pl.pallas_call(
        functools.partial(join_kernel, [len(part) for part in parts]),
        out_shape=jax.ShapeDtypeStruct((3, share, columns), jnp.bfloat16),
        compiler_params=pltpu.CompilerParams(vmem_limit_bytes=16 * 2**20),
        name="join",
    )(*[state for part in parts for state in part])


def swap(states, groups, step):
    moved = [
        lax.ppermute(state, "gz", [(i, i ^ (k * step)) for i in range(groups)]) for k, state in enumerate(states) if k
    ]
    return [states[0]] + moved


def per_device(planes, level_gain):
    columns = planes.shape[3]
    tiles = lax.axis_size("tile")
    groups = lax.axis_size("gz")
    slow = min(4, groups)
    fast = groups // slow
    split = 5 * columns // 8
    to_core, to_far = edge_luminance(planes)
    core = lax.ppermute(to_core, "tile", [(i, i ^ 1) for i in range(tiles)])
    between = range(1, tiles - 1, 2)
    far = lax.ppermute(to_far, "tile", [(i, i + 1) for i in between] + [(i + 1, i) for i in between])
    own = own_rows(planes, tiles)
    states = local_state(own, core, far, level_gain, slow, groups, split)
    first = swap(states[:fast], groups, 1)
    second = swap(states[fast:], groups, fast)
    first = swap(merge(first, lambda group: group // fast), groups, fast)
    second = swap(merge(second, lambda group: group % fast), groups, 1)
    return join(first, second)


def solution(mesh):
    return jax.shard_map(
        per_device,
        mesh=mesh,
        in_specs=(P("gz", None, "tile", None), P()),
        out_specs=P(None, ("tile", "gz"), None),
        check_vma=False,
    )
```

```python
import functools

import jax
import jax.numpy as jnp
import numpy as np
from jax import lax
from jax.experimental import pallas as pl
from jax.experimental.pallas import tpu as pltpu
from jax.sharding import PartitionSpec as P

LEVELS = 4
TAPS = (1, 4, 6, 4, 1)
HALO = 32
LANES = 128
WINDOW = 256
STEP = 192


def band_products(count):
    made = []
    whole = np.eye(count)
    for level in range(LEVELS):
        step = sum(tap * np.eye(count, k=(place - 2) * 2**level) for place, tap in enumerate(TAPS))
        whole = step @ whole
        made.append(whole)
    return made


def split_exact(matrix):
    high = matrix.astype(jnp.bfloat16).astype(matrix.dtype)
    return high, matrix - high


def row_matrices(image_rows, rows):
    bands = band_products(image_rows)

    def taps(lines, first, last):
        parts = []
        for level, band in enumerate(bands):
            high, low = split_exact(np.pad(band, ((0, 0), (HALO, HALO)))[lines, first + HALO : last + HALO])
            scale = 1.0 / 16 ** (level + 1)
            parts.append(high * scale)
            if level >= 2:
                parts.append(low * scale)
        return np.concatenate(parts, axis=0)

    inner = np.arange(HALO, rows - HALO)
    edge = np.concatenate([np.arange(HALO), np.arange(rows - HALO, rows)])
    starts = [tile * rows for tile in (0, 1, image_rows // rows - 1)]
    return (
        taps(rows + inner, rows, 2 * rows).astype(jnp.bfloat16),
        np.stack([taps(start + edge, start - HALO, start + rows + HALO) for start in starts]).astype(jnp.bfloat16),
    )


def windows_of(columns):
    count = (columns - WINDOW) // STEP + 1
    assert (count - 1) * STEP + WINDOW == columns
    inside = [STEP * k + HALO for k in range(1, count)]
    return list(zip([0] + inside, inside + [columns]))


def column_matrices(columns):
    split = [split_exact(band) for band in band_products(columns)]
    parts = [high / 16 ** (level + 1) for level, (high, _) in enumerate(split)]
    parts += [low / 16 ** (level + 1) for level, (_, low) in enumerate(split) if level >= 2]
    made = np.zeros((len(windows_of(columns)), len(parts), WINDOW, WINDOW))
    for k, (first, last) in enumerate(windows_of(columns)):
        inputs, outputs = np.arange(STEP * k, STEP * k + WINDOW), np.arange(first, last)
        for j, part in enumerate(parts):
            made[k, j][np.ix_(inputs % WINDOW, outputs % WINDOW)] = part[np.ix_(outputs, inputs)].T
    return made.astype(jnp.bfloat16)


def filters(columns, rows, tiles):
    inner, edge = row_matrices(rows * tiles, rows)
    parts = [column_matrices(columns).reshape(-1, WINDOW)]
    for part in (inner, *edge):
        parts.append(np.pad(part, ((0, 0), (0, WINDOW - part.shape[1]))))
    return np.concatenate(parts, axis=0)


def dot(left, right):
    return jnp.dot(left, right, preferred_element_type=jnp.float32)


def luminance_of(colours):
    red, green, blue = (colours[channel].astype(jnp.float32) for channel in range(3))
    return (0.299 * red + 0.587 * green + 0.114 * blue).astype(jnp.bfloat16)


def combine(states):
    states = [[part.astype(jnp.float32) for part in state] for state in states]
    peak = functools.reduce(jnp.maximum, [state[0] for state in states])
    weights = [state[1] * jnp.exp(state[0] - peak) for state in states]
    total = sum(weights[1:], weights[0])
    inverse = 1.0 / total
    colours = []
    for channel in range(2, 5):
        terms = [weight * state[channel] for weight, state in zip(weights, states)]
        colours.append(sum(terms[1:], terms[0]) * inverse)
    return [peak, total] + colours


def fetch_kernel(planes_ref, stack_ref, core_ref, far_ref, arrived):
    depth, _, rows, _ = planes_ref.shape
    odd = lax.axis_index("tile") % 2
    copies = []
    for part, (start, count) in enumerate(((0, HALO), (rows - HALO, HALO), (HALO, rows - 2 * HALO))):
        at = pl.ds(start, count)
        copies.append(pltpu.make_async_copy(planes_ref.at[:, :, at], stack_ref.at[:, :, at], arrived.at[part]))
        copies[-1].start()
    copies[0].wait()
    copies[1].wait()
    tail, head = rows - HALO, 0
    for out, start in ((core_ref, jnp.where(odd == 0, tail, head)), (far_ref, jnp.where(odd == 0, head, tail))):
        at = pl.ds(pl.multiple_of(start, HALO), HALO)
        for plane in range(depth):
            out[plane] = luminance_of([stack_ref[plane, channel, at] for channel in range(3)])
    copies[2].wait()


def fetch(planes):
    depth, _, _, columns = planes.shape
    vmem = pl.BlockSpec(memory_space=pltpu.VMEM)
    shapes = [planes.shape] + [(depth, HALO, columns)] * 2
    return pl.pallas_call(
        fetch_kernel,
        out_shape=[jax.ShapeDtypeStruct(shape, jnp.bfloat16) for shape in shapes],
        in_specs=[pl.BlockSpec(memory_space=pl.ANY)],
        out_specs=[vmem] * 3,
        scratch_shapes=[pltpu.SemaphoreType.DMA((3,))],
        compiler_params=pltpu.CompilerParams(vmem_limit_bytes=50 * 2**20),
        name="fetch",
    )(planes)


def lane_below(limit, rows):
    return lax.broadcasted_iota(jnp.int32, (rows, LANES), 1) < limit


def filter_rows(row_ref, reach, window_of, depth, columns, high, low):
    count = row_ref.shape[0] // 6
    below = lane_below(LANES // 2, count)
    for plane in range(depth):
        here = pl.ds(plane * count, count)
        smooth = [dot(row_ref[:, :reach], window_of(plane, pl.ds(at, WINDOW))) for at in range(0, columns, WINDOW)]
        for level, parts in enumerate(((0,), (1,), (2, 3), (4, 5))):
            value = [sum(field[k * count : (k + 1) * count] for k in parts) for field in smooth]
            value = [half for field in value for half in (field[:, :LANES], field[:, LANES:])]
            for window in range(len(windows_of(columns))):
                first, mixed = divmod(STEP * window, LANES)
                for group in (first, first + 1):
                    line = value[group]
                    if mixed and group == first:
                        line = jnp.where(below, value[group + 2], line)
                    at = pl.ds(window * WINDOW + group % 2 * LANES, LANES)
                    top = line.astype(jnp.bfloat16)
                    high[level, here, at] = top
                    low[level, here, at] = (line - top.astype(jnp.float32)).astype(jnp.bfloat16)


def smooth_window(window, col_ref, high, low):
    at = pl.ds(window * WINDOW, WINDOW)
    made = []
    for level in range(LEVELS):
        top, rest = high[level, :, at], low[level, :, at]
        taps = [col_ref[pl.ds((window * 6 + k) * WINDOW, WINDOW)] for k in ((level,) if level < 2 else (level, level + 2))]
        value = dot(top, taps[0]) + dot(rest, taps[0])
        if level >= 2:
            value = value + dot(top, taps[1])
        made.append(value)
    return made


def scores(columns, luminance_at, gain_ref, col_ref, high, low):
    before = None
    ends = windows_of(columns)
    for window, (_, end) in enumerate(ends):
        after = smooth_window(window, col_ref, high, low)
        start = 0 if window == 0 else ends[window - 1][1] // LANES
        for group in range(start, end // LANES):
            at = pl.ds(group * LANES, LANES)
            half = slice(group % 2 * LANES, (group % 2 + 1) * LANES)
            approx = luminance_at(at).astype(jnp.float32)
            approx = approx.reshape(-1, LANES)
            score = jnp.zeros(approx.shape, jnp.float32)
            border = 0 if window == 0 else ends[window - 1][1] - group * LANES
            for level in range(LEVELS):
                smoother = after[level][:, half]
                if border > 0:
                    smoother = jnp.where(lane_below(border, smoother.shape[0]), before[level][:, half], smoother)
                detail = approx - smoother
                score = score + gain_ref[level] * detail * detail
                approx = smoother
            yield at, score
        before = after


def state_of(score, colours):
    peak = jnp.max(score, axis=0).astype(jnp.bfloat16)
    weight = jnp.exp(score - peak.astype(jnp.float32)[None])
    total = jnp.sum(weight, axis=0)
    inverse = 1.0 / total
    means = [jnp.sum(weight * colour.astype(jnp.float32), axis=0) * inverse for colour in colours]
    return [peak, total.astype(jnp.bfloat16)] + [mean.astype(jnp.bfloat16) for mean in means]


def inner_kernel(
    gain_ref, planes_ref, taps_ref, lum_ref, row_ref, col_ref, state_ref, spread_ref, gain, inner, high, low, arrived
):
    depth, _, rows, columns = planes_ref.shape
    bands, _, share, _ = state_ref.shape
    count = rows - 2 * HALO
    tile, tiles = lax.axis_index("tile"), lax.axis_size("tile")
    tile_case = jnp.where(tile == 0, 0, jnp.where(tile == tiles - 1, 2, 1))
    lines, first = inner.shape[0], col_ref.shape[0]
    edge = pl.multiple_of(first + lines + tile_case * row_ref.shape[0], LANES)
    copies = []
    copies.append(pltpu.make_async_copy(gain_ref, gain, arrived.at[0]))
    copies[0].start()
    for start, target in ((first, inner), (0, col_ref), (edge, row_ref)):
        source = taps_ref.at[pl.ds(start, target.shape[0])]
        copies.append(pltpu.make_async_copy(source, target, arrived.at[len(copies)]))
        copies[-1].start()
    for plane in range(depth):
        lum_ref[plane] = luminance_of([planes_ref[plane, channel] for channel in range(3)])
    copies[1].wait()
    filter_rows(inner, rows, lambda plane, at: lum_ref[plane, :, at], depth, columns, high, low)
    copies[0].wait()
    for level in range(LEVELS):
        spread_ref[level] = jnp.full((1, LANES), gain[level], jnp.float32)
    copies[2].wait()
    inside = pl.ds(HALO, count)
    for at, score in scores(columns, lambda at: lum_ref[:, inside, at], gain, col_ref, high, low):
        colours = [planes_ref[:, channel, inside, at] for channel in range(3)]
        for k, part in enumerate(state_of(score.reshape(depth, count, LANES), colours)):
            state_ref[:, k, :, at] = part.reshape(bands, share, LANES)
    copies[3].wait()


def inner_state(planes, level_gain, groups, tiles):
    depth, channels, rows, columns = planes.shape
    count, share = rows - 2 * HALO, rows // groups
    taps = jnp.asarray(filters(columns, rows, tiles))
    inner_lines, edge_lines = 6 * count, 12 * HALO
    vmem = pl.BlockSpec(memory_space=pltpu.VMEM)
    window_lines = taps.shape[0] - inner_lines - 3 * edge_lines
    shapes = [(depth, rows, columns), (edge_lines, WINDOW), (window_lines, WINDOW), (count // share, 5, share, columns)]
    wide = len(windows_of(columns)) * WINDOW
    return pl.pallas_call(
        inner_kernel,
        out_shape=[jax.ShapeDtypeStruct(shape, jnp.bfloat16) for shape in shapes]
        + [jax.ShapeDtypeStruct((LEVELS, 1, LANES), jnp.float32)],
        in_specs=[pl.BlockSpec(memory_space=pl.ANY), vmem, pl.BlockSpec(memory_space=pl.ANY)],
        out_specs=[vmem] * (len(shapes) + 1),
        scratch_shapes=[
            pltpu.SMEM((LEVELS,), jnp.float32),
            pltpu.VMEM((inner_lines, WINDOW), jnp.bfloat16),
            pltpu.VMEM((LEVELS, depth * count, wide), jnp.bfloat16),
            pltpu.VMEM((LEVELS, depth * count, wide), jnp.bfloat16),
            pltpu.SemaphoreType.DMA((4,)),
        ],
        compiler_params=pltpu.CompilerParams(vmem_limit_bytes=43 * 2**20),
        cost_estimate=pl.CostEstimate(flops=2**30, bytes_accessed=10 * 2**20, transcendentals=0),
        name="inner_state",
    )(level_gain, planes, taps)


def edge_state_kernel(slow, planes_ref, lum_ref, row_ref, col_ref, inner_ref, gain_ref, core_ref, far_ref, *refs):
    *outs, halo, high, low, held = refs
    depth, _, rows, columns = planes_ref.shape
    groups, _, share, _ = held.shape
    fast = groups // slow
    split = outs[0].shape[-1]
    odd = lax.axis_index("tile") % 2

    def place_halo(above_ref, below_ref):
        halo[0] = above_ref[...]
        halo[1] = below_ref[...]

    pl.when(odd == 0)(lambda: place_halo(far_ref, core_ref))
    pl.when(odd == 1)(lambda: place_halo(core_ref, far_ref))

    def window_of(plane, at):
        return jnp.concatenate([halo[0, plane, :, at], lum_ref[plane, :, at], halo[1, plane, :, at]], axis=0)

    def edges_of(ref, *index):
        return jnp.concatenate([ref[index[:-1] + (pl.ds(start, HALO), index[-1])] for start in (0, rows - HALO)], axis=-2)

    filter_rows(row_ref, rows + 2 * HALO, window_of, depth, columns, high, low)
    side = HALO // share
    held[side : groups - side] = inner_ref[...]
    for at, score in scores(columns, lambda at: edges_of(lum_ref, slice(None), at), gain_ref, col_ref, high, low):
        colours = [edges_of(planes_ref, slice(None), channel, at) for channel in range(3)]
        for k, part in enumerate(state_of(score.reshape(depth, 2 * HALO, LANES), colours)):
            held[:side, k, :, at] = part[:HALO].reshape(side, share, LANES)
            held[groups - side :, k, :, at] = part[HALO:].reshape(side, share, LANES)

    group = lax.axis_index("gz")
    mine_slow, mine_fast = group // fast, group % fast
    for other in range(fast):
        for place in range(slow):
            outs[other][place] = held[place * fast + (mine_fast ^ other), :, :, :split]
    for other in range(slow):
        for place in range(fast):
            outs[fast + other][place] = held[(mine_slow ^ other) * fast + place, :, :, split:]


def edge_state(planes, inner, core, far, slow, groups, split):
    depth, _, rows, columns = planes.shape
    fast, share = groups // slow, rows // groups
    vmem = pl.BlockSpec(memory_space=pltpu.VMEM)
    wide = len(windows_of(columns)) * WINDOW
    shapes = [(slow, 5, share, split)] * fast + [(fast, 5, share, columns - split)] * slow
    return pl.pallas_call(
        functools.partial(edge_state_kernel, slow),
        out_shape=[jax.ShapeDtypeStruct(shape, jnp.bfloat16) for shape in shapes],
        in_specs=[vmem] * 8,
        out_specs=[vmem] * len(shapes),
        scratch_shapes=[
            pltpu.VMEM((2, depth, HALO, columns), jnp.bfloat16),
            pltpu.VMEM((LEVELS, 2 * depth * HALO, wide), jnp.bfloat16),
            pltpu.VMEM((LEVELS, 2 * depth * HALO, wide), jnp.bfloat16),
            pltpu.VMEM((groups, 5, share, columns), jnp.bfloat16),
        ],
        compiler_params=pltpu.CompilerParams(vmem_limit_bytes=40 * 2**20),
        name="edge_state",
    )(planes, *inner, core, far)


def merge_kernel(count, pick, *refs):
    states, outs, held = refs[:count], refs[count:-1], refs[-1]
    for place in range(held.shape[0]):
        for k, part in enumerate(combine([[state[place, k] for k in range(5)] for state in states])):
            held[place, k] = part.astype(jnp.bfloat16)
    place = pick(lax.axis_index("gz"))
    for other, out in enumerate(outs):
        out[...] = held[place ^ other]


def merge(states, pick):
    bands, _, share, columns = states[0].shape
    return pl.pallas_call(
        functools.partial(merge_kernel, len(states), pick),
        out_shape=[jax.ShapeDtypeStruct((5, share, columns), jnp.bfloat16)] * bands,
        scratch_shapes=[pltpu.VMEM(states[0].shape, jnp.bfloat16)],
        compiler_params=pltpu.CompilerParams(vmem_limit_bytes=16 * 2**20),
        name="merge",
    )(*states)


def join_kernel(counts, *refs):
    *refs, out_ref = refs
    start = 0
    for count in counts:
        states, refs = refs[:count], refs[count:]
        width = states[0].shape[-1]
        merged = combine([[state[k] for k in range(5)] for state in states])
        for channel in range(3):
            out_ref[channel, :, start : start + width] = merged[2 + channel].astype(jnp.bfloat16)
        start += width


def join(*parts):
    share = parts[0][0].shape[1]
    columns = sum(part[0].shape[2] for part in parts)
    return pl.pallas_call(
        functools.partial(join_kernel, [len(part) for part in parts]),
        out_shape=jax.ShapeDtypeStruct((3, share, columns), jnp.bfloat16),
        compiler_params=pltpu.CompilerParams(vmem_limit_bytes=16 * 2**20),
        name="join",
    )(*[state for part in parts for state in part])


def swap(states, groups, step):
    moved = [
        lax.ppermute(state, "gz", [(i, i ^ (k * step)) for i in range(groups)]) for k, state in enumerate(states) if k
    ]
    return [states[0]] + moved


def per_device(planes, level_gain):
    columns = planes.shape[3]
    tiles = lax.axis_size("tile")
    groups = lax.axis_size("gz")
    slow = min(4, groups)
    fast = groups // slow
    split = 5 * columns // 8
    stack, to_core, to_far = fetch(planes)
    core = lax.ppermute(to_core, "tile", [(i, i ^ 1) for i in range(tiles)])
    between = range(1, tiles - 1, 2)
    far = lax.ppermute(to_far, "tile", [(i, i + 1) for i in between] + [(i + 1, i) for i in between])
    inner = inner_state(stack, level_gain, groups, tiles)
    states = edge_state(stack, inner, core, far, slow, groups, split)
    first = swap(states[:fast], groups, 1)
    second = swap(states[fast:], groups, fast)
    first = swap(merge(first, lambda group: group // fast), groups, fast)
    second = swap(merge(second, lambda group: group % fast), groups, 1)
    return join(first, second)


def solution(mesh):
    return jax.shard_map(
        per_device,
        mesh=mesh,
        in_specs=(P("gz", None, "tile", None), P()),
        out_specs=P(None, ("tile", "gz"), None),
        check_vma=False,
    )
```

```python
import functools

import jax
import jax.numpy as jnp
import numpy as np
from jax import lax
from jax.experimental import pallas as pl
from jax.experimental.pallas import tpu as pltpu
from jax.sharding import PartitionSpec as P

LEVELS = 4
TAPS = (1, 4, 6, 4, 1)
HALO = 32
LANES = 128
WINDOW = 256
STEP = 192


def band_products(count):
    made = []
    whole = np.eye(count)
    for level in range(LEVELS):
        step = sum(tap * np.eye(count, k=(place - 2) * 2**level) for place, tap in enumerate(TAPS))
        whole = step @ whole
        made.append(whole)
    return made


def split_exact(matrix):
    high = matrix.astype(jnp.bfloat16).astype(matrix.dtype)
    return high, matrix - high


def row_matrices(image_rows, rows):
    bands = band_products(image_rows)

    def taps(lines, first, last):
        parts = []
        for level, band in enumerate(bands):
            high, low = split_exact(np.pad(band, ((0, 0), (HALO, HALO)))[lines, first + HALO : last + HALO])
            scale = 1.0 / 16 ** (level + 1)
            parts.append(high * scale)
            if level >= 2:
                parts.append(low * scale)
        return np.concatenate(parts, axis=0)

    inner = np.arange(HALO, rows - HALO)
    edge = np.concatenate([np.arange(HALO), np.arange(rows - HALO, rows)])
    starts = [tile * rows for tile in (0, 1, image_rows // rows - 1)]
    return (
        taps(rows + inner, rows, 2 * rows).astype(jnp.bfloat16),
        np.stack([taps(start + edge, start - HALO, start + rows + HALO) for start in starts]).astype(jnp.bfloat16),
    )


def windows_of(columns):
    count = (columns - WINDOW) // STEP + 1
    assert (count - 1) * STEP + WINDOW == columns
    inside = [STEP * k + HALO for k in range(1, count)]
    return list(zip([0] + inside, inside + [columns]))


def column_matrices(columns):
    split = [split_exact(band) for band in band_products(columns)]
    parts = [high / 16 ** (level + 1) for level, (high, _) in enumerate(split)]
    parts += [low / 16 ** (level + 1) for level, (_, low) in enumerate(split) if level >= 2]
    made = np.zeros((len(windows_of(columns)), len(parts), WINDOW, WINDOW))
    for k, (first, last) in enumerate(windows_of(columns)):
        inputs, outputs = np.arange(STEP * k, STEP * k + WINDOW), np.arange(first, last)
        for j, part in enumerate(parts):
            made[k, j][np.ix_(inputs % WINDOW, outputs % WINDOW)] = part[np.ix_(outputs, inputs)].T
    return made.astype(jnp.bfloat16)


def filters(columns, rows, tiles):
    inner, edge = row_matrices(rows * tiles, rows)
    parts = [column_matrices(columns).reshape(-1, WINDOW)]
    for part in (inner, *edge):
        parts.append(np.pad(part, ((0, 0), (0, WINDOW - part.shape[1]))))
    return np.concatenate(parts, axis=0)


def dot(left, right):
    return jnp.dot(left, right, preferred_element_type=jnp.float32)


def luminance_of(colours):
    red, green, blue = (colours[channel].astype(jnp.float32) for channel in range(3))
    return (0.299 * red + 0.587 * green + 0.114 * blue).astype(jnp.bfloat16)


def combine(states):
    states = [[part.astype(jnp.float32) for part in state] for state in states]
    peak = functools.reduce(jnp.maximum, [state[0] for state in states])
    weights = [state[1] * jnp.exp(state[0] - peak) for state in states]
    total = sum(weights[1:], weights[0])
    inverse = 1.0 / total
    colours = []
    for channel in range(2, 5):
        terms = [weight * state[channel] for weight, state in zip(weights, states)]
        colours.append(sum(terms[1:], terms[0]) * inverse)
    return [peak, total] + colours


def fetch_kernel(planes_ref, stack_ref, core_ref, far_ref, arrived):
    depth, _, rows, _ = planes_ref.shape
    odd = lax.axis_index("tile") % 2
    copies = []
    for part, (start, count) in enumerate(((0, HALO), (rows - HALO, HALO), (HALO, rows - 2 * HALO))):
        at = pl.ds(start, count)
        copies.append(pltpu.make_async_copy(planes_ref.at[:, :, at], stack_ref.at[:, :, at], arrived.at[part]))
        copies[-1].start()
    copies[0].wait()
    copies[1].wait()
    tail, head = rows - HALO, 0
    for out, start in ((core_ref, jnp.where(odd == 0, tail, head)), (far_ref, jnp.where(odd == 0, head, tail))):
        at = pl.ds(pl.multiple_of(start, HALO), HALO)
        for plane in range(depth):
            out[plane] = luminance_of([stack_ref[plane, channel, at] for channel in range(3)])
    copies[2].wait()


def fetch(planes):
    depth, _, _, columns = planes.shape
    vmem = pl.BlockSpec(memory_space=pltpu.VMEM)
    shapes = [planes.shape] + [(depth, HALO, columns)] * 2
    return pl.pallas_call(
        fetch_kernel,
        out_shape=[jax.ShapeDtypeStruct(shape, jnp.bfloat16) for shape in shapes],
        in_specs=[pl.BlockSpec(memory_space=pl.ANY)],
        out_specs=[vmem] * 3,
        scratch_shapes=[pltpu.SemaphoreType.DMA((3,))],
        compiler_params=pltpu.CompilerParams(vmem_limit_bytes=50 * 2**20),
        cost_estimate=pl.CostEstimate(flops=2**32, bytes_accessed=64 * 2**20, transcendentals=0),
        name="fetch",
    )(planes)


def lane_below(limit, rows):
    return lax.broadcasted_iota(jnp.int32, (rows, LANES), 1) < limit


def filter_rows(row_ref, reach, window_of, depth, columns, high, low):
    count = row_ref.shape[0] // 6
    below = lane_below(LANES // 2, count)
    for plane in range(depth):
        here = pl.ds(plane * count, count)
        smooth = [dot(row_ref[:, :reach], window_of(plane, pl.ds(at, WINDOW))) for at in range(0, columns, WINDOW)]
        for level, parts in enumerate(((0,), (1,), (2, 3), (4, 5))):
            value = [sum(field[k * count : (k + 1) * count] for k in parts) for field in smooth]
            value = [half for field in value for half in (field[:, :LANES], field[:, LANES:])]
            for window in range(len(windows_of(columns))):
                first, mixed = divmod(STEP * window, LANES)
                for group in (first, first + 1):
                    line = value[group]
                    if mixed and group == first:
                        line = jnp.where(below, value[group + 2], line)
                    at = pl.ds(window * WINDOW + group % 2 * LANES, LANES)
                    top = line.astype(jnp.bfloat16)
                    high[level, here, at] = top
                    low[level, here, at] = (line - top.astype(jnp.float32)).astype(jnp.bfloat16)


def smooth_window(window, col_ref, high, low):
    at = pl.ds(window * WINDOW, WINDOW)
    made = []
    for level in range(LEVELS):
        top, rest = high[level, :, at], low[level, :, at]
        taps = [col_ref[pl.ds((window * 6 + k) * WINDOW, WINDOW)] for k in ((level,) if level < 2 else (level, level + 2))]
        value = dot(top, taps[0]) + dot(rest, taps[0])
        if level >= 2:
            value = value + dot(top, taps[1])
        made.append(value)
    return made


def scores(columns, luminance_at, gain_ref, col_ref, high, low):
    before = None
    ends = windows_of(columns)
    for window, (_, end) in enumerate(ends):
        after = smooth_window(window, col_ref, high, low)
        start = 0 if window == 0 else ends[window - 1][1] // LANES
        for group in range(start, end // LANES):
            at = pl.ds(group * LANES, LANES)
            half = slice(group % 2 * LANES, (group % 2 + 1) * LANES)
            approx = luminance_at(at).astype(jnp.float32)
            approx = approx.reshape(-1, LANES)
            score = jnp.zeros(approx.shape, jnp.float32)
            border = 0 if window == 0 else ends[window - 1][1] - group * LANES
            for level in range(LEVELS):
                smoother = after[level][:, half]
                if border > 0:
                    smoother = jnp.where(lane_below(border, smoother.shape[0]), before[level][:, half], smoother)
                detail = approx - smoother
                score = score + gain_ref[level] * detail * detail
                approx = smoother
            yield at, score
        before = after


def state_of(score, colours):
    peak = jnp.max(score, axis=0).astype(jnp.bfloat16)
    weight = jnp.exp(score - peak.astype(jnp.float32)[None])
    total = jnp.sum(weight, axis=0)
    inverse = 1.0 / total
    means = [jnp.sum(weight * colour.astype(jnp.float32), axis=0) * inverse for colour in colours]
    return [peak, total.astype(jnp.bfloat16)] + [mean.astype(jnp.bfloat16) for mean in means]


def inner_kernel(
    gain_ref, planes_ref, taps_ref, lum_ref, row_ref, col_ref, state_ref, spread_ref, gain, inner, high, low, arrived
):
    depth, _, rows, columns = planes_ref.shape
    bands, _, share, _ = state_ref.shape
    count = rows - 2 * HALO
    tile, tiles = lax.axis_index("tile"), lax.axis_size("tile")
    tile_case = jnp.where(tile == 0, 0, jnp.where(tile == tiles - 1, 2, 1))
    lines, first = inner.shape[0], col_ref.shape[0]
    edge = pl.multiple_of(first + lines + tile_case * row_ref.shape[0], LANES)
    copies = []
    copies.append(pltpu.make_async_copy(gain_ref, gain, arrived.at[0]))
    copies[0].start()
    for start, target in ((first, inner), (0, col_ref), (edge, row_ref)):
        source = taps_ref.at[pl.ds(start, target.shape[0])]
        copies.append(pltpu.make_async_copy(source, target, arrived.at[len(copies)]))
        copies[-1].start()
    for plane in range(depth):
        lum_ref[plane] = luminance_of([planes_ref[plane, channel] for channel in range(3)])
    copies[1].wait()
    filter_rows(inner, rows, lambda plane, at: lum_ref[plane, :, at], depth, columns, high, low)
    copies[0].wait()
    for level in range(LEVELS):
        spread_ref[level] = jnp.full((1, LANES), gain[level], jnp.float32)
    copies[2].wait()
    inside = pl.ds(HALO, count)
    for at, score in scores(columns, lambda at: lum_ref[:, inside, at], gain, col_ref, high, low):
        colours = [planes_ref[:, channel, inside, at] for channel in range(3)]
        for k, part in enumerate(state_of(score.reshape(depth, count, LANES), colours)):
            state_ref[:, k, :, at] = part.reshape(bands, share, LANES)
    copies[3].wait()


def inner_state(planes, level_gain, groups, tiles):
    depth, channels, rows, columns = planes.shape
    count, share = rows - 2 * HALO, rows // groups
    taps = jnp.asarray(filters(columns, rows, tiles))
    inner_lines, edge_lines = 6 * count, 12 * HALO
    vmem = pl.BlockSpec(memory_space=pltpu.VMEM)
    window_lines = taps.shape[0] - inner_lines - 3 * edge_lines
    shapes = [(depth, rows, columns), (edge_lines, WINDOW), (window_lines, WINDOW), (count // share, 5, share, columns)]
    wide = len(windows_of(columns)) * WINDOW
    return pl.pallas_call(
        inner_kernel,
        out_shape=[jax.ShapeDtypeStruct(shape, jnp.bfloat16) for shape in shapes]
        + [jax.ShapeDtypeStruct((LEVELS, 1, LANES), jnp.float32)],
        in_specs=[pl.BlockSpec(memory_space=pl.ANY), vmem, pl.BlockSpec(memory_space=pl.ANY)],
        out_specs=[vmem] * (len(shapes) + 1),
        scratch_shapes=[
            pltpu.SMEM((LEVELS,), jnp.float32),
            pltpu.VMEM((inner_lines, WINDOW), jnp.bfloat16),
            pltpu.VMEM((LEVELS, depth * count, wide), jnp.bfloat16),
            pltpu.VMEM((LEVELS, depth * count, wide), jnp.bfloat16),
            pltpu.SemaphoreType.DMA((4,)),
        ],
        compiler_params=pltpu.CompilerParams(vmem_limit_bytes=43 * 2**20),
        cost_estimate=pl.CostEstimate(flops=2**30, bytes_accessed=10 * 2**20, transcendentals=0),
        name="inner_state",
    )(level_gain, planes, taps)


def edge_state_kernel(slow, planes_ref, lum_ref, row_ref, col_ref, inner_ref, gain_ref, core_ref, far_ref, *refs):
    *outs, halo, high, low, held = refs
    depth, _, rows, columns = planes_ref.shape
    groups, _, share, _ = held.shape
    fast = groups // slow
    split = outs[0].shape[-1]
    odd = lax.axis_index("tile") % 2

    def place_halo(above_ref, below_ref):
        halo[0] = above_ref[...]
        halo[1] = below_ref[...]

    pl.when(odd == 0)(lambda: place_halo(far_ref, core_ref))
    pl.when(odd == 1)(lambda: place_halo(core_ref, far_ref))

    def window_of(plane, at):
        return jnp.concatenate([halo[0, plane, :, at], lum_ref[plane, :, at], halo[1, plane, :, at]], axis=0)

    def edges_of(ref, *index):
        return jnp.concatenate([ref[index[:-1] + (pl.ds(start, HALO), index[-1])] for start in (0, rows - HALO)], axis=-2)

    filter_rows(row_ref, rows + 2 * HALO, window_of, depth, columns, high, low)
    side = HALO // share
    held[side : groups - side] = inner_ref[...]
    for at, score in scores(columns, lambda at: edges_of(lum_ref, slice(None), at), gain_ref, col_ref, high, low):
        colours = [edges_of(planes_ref, slice(None), channel, at) for channel in range(3)]
        for k, part in enumerate(state_of(score.reshape(depth, 2 * HALO, LANES), colours)):
            held[:side, k, :, at] = part[:HALO].reshape(side, share, LANES)
            held[groups - side :, k, :, at] = part[HALO:].reshape(side, share, LANES)

    group = lax.axis_index("gz")
    mine_slow, mine_fast = group // fast, group % fast
    for other in range(fast):
        for place in range(slow):
            outs[other][place] = held[place * fast + (mine_fast ^ other), :, :, :split]
    for other in range(slow):
        for place in range(fast):
            outs[fast + other][place] = held[(mine_slow ^ other) * fast + place, :, :, split:]


def edge_state(planes, inner, core, far, slow, groups, split):
    depth, _, rows, columns = planes.shape
    fast, share = groups // slow, rows // groups
    vmem = pl.BlockSpec(memory_space=pltpu.VMEM)
    wide = len(windows_of(columns)) * WINDOW
    shapes = [(slow, 5, share, split)] * fast + [(fast, 5, share, columns - split)] * slow
    return pl.pallas_call(
        functools.partial(edge_state_kernel, slow),
        out_shape=[jax.ShapeDtypeStruct(shape, jnp.bfloat16) for shape in shapes],
        in_specs=[vmem] * 8,
        out_specs=[vmem] * len(shapes),
        scratch_shapes=[
            pltpu.VMEM((2, depth, HALO, columns), jnp.bfloat16),
            pltpu.VMEM((LEVELS, 2 * depth * HALO, wide), jnp.bfloat16),
            pltpu.VMEM((LEVELS, 2 * depth * HALO, wide), jnp.bfloat16),
            pltpu.VMEM((groups, 5, share, columns), jnp.bfloat16),
        ],
        compiler_params=pltpu.CompilerParams(vmem_limit_bytes=40 * 2**20),
        name="edge_state",
    )(planes, *inner, core, far)


def merge_kernel(count, pick, *refs):
    states, outs, held = refs[:count], refs[count:-1], refs[-1]
    for place in range(held.shape[0]):
        for k, part in enumerate(combine([[state[place, k] for k in range(5)] for state in states])):
            held[place, k] = part.astype(jnp.bfloat16)
    place = pick(lax.axis_index("gz"))
    for other, out in enumerate(outs):
        out[...] = held[place ^ other]


def merge(states, pick):
    bands, _, share, columns = states[0].shape
    return pl.pallas_call(
        functools.partial(merge_kernel, len(states), pick),
        out_shape=[jax.ShapeDtypeStruct((5, share, columns), jnp.bfloat16)] * bands,
        scratch_shapes=[pltpu.VMEM(states[0].shape, jnp.bfloat16)],
        compiler_params=pltpu.CompilerParams(vmem_limit_bytes=16 * 2**20),
        name="merge",
    )(*states)


def join_kernel(counts, *refs):
    *refs, out_ref = refs
    start = 0
    for count in counts:
        states, refs = refs[:count], refs[count:]
        width = states[0].shape[-1]
        merged = combine([[state[k] for k in range(5)] for state in states])
        for channel in range(3):
            out_ref[channel, :, start : start + width] = merged[2 + channel].astype(jnp.bfloat16)
        start += width


def join(*parts):
    share = parts[0][0].shape[1]
    columns = sum(part[0].shape[2] for part in parts)
    return pl.pallas_call(
        functools.partial(join_kernel, [len(part) for part in parts]),
        out_shape=jax.ShapeDtypeStruct((3, share, columns), jnp.bfloat16),
        compiler_params=pltpu.CompilerParams(vmem_limit_bytes=16 * 2**20),
        name="join",
    )(*[state for part in parts for state in part])


def swap(states, groups, step):
    moved = [
        lax.ppermute(state, "gz", [(i, i ^ (k * step)) for i in range(groups)]) for k, state in enumerate(states) if k
    ]
    return [states[0]] + moved


def per_device(planes, level_gain):
    columns = planes.shape[3]
    tiles = lax.axis_size("tile")
    groups = lax.axis_size("gz")
    slow = min(4, groups)
    fast = groups // slow
    split = 5 * columns // 8
    stack, to_core, to_far = fetch(planes)
    core = lax.ppermute(to_core, "tile", [(i, i ^ 1) for i in range(tiles)])
    between = range(1, tiles - 1, 2)
    far = lax.ppermute(to_far, "tile", [(i, i + 1) for i in between] + [(i + 1, i) for i in between])
    inner = inner_state(stack, level_gain, groups, tiles)
    states = edge_state(stack, inner, core, far, slow, groups, split)
    first = swap(states[:fast], groups, 1)
    second = swap(states[fast:], groups, fast)
    first = swap(merge(first, lambda group: group // fast), groups, fast)
    second = swap(merge(second, lambda group: group % fast), groups, 1)
    return join(first, second)


def solution(mesh):
    return jax.shard_map(
        per_device,
        mesh=mesh,
        in_specs=(P("gz", None, "tile", None), P()),
        out_specs=P(None, ("tile", "gz"), None),
        check_vma=False,
    )
```

```python
import functools

import jax
import jax.numpy as jnp
import numpy as np
from jax import lax
from jax.experimental import pallas as pl
from jax.experimental.pallas import tpu as pltpu
from jax.sharding import PartitionSpec as P

LEVELS = 4
TAPS = (1, 4, 6, 4, 1)
HALO = 32
LANES = 128
WINDOW = 256
STEP = 192
FAR_FIRST = (3, 1, 2)


def band_products(count):
    made = []
    whole = np.eye(count)
    for level in range(LEVELS):
        step = sum(tap * np.eye(count, k=(place - 2) * 2**level) for place, tap in enumerate(TAPS))
        whole = step @ whole
        made.append(whole)
    return made


def split_exact(matrix):
    high = matrix.astype(jnp.bfloat16).astype(matrix.dtype)
    return high, matrix - high


def row_matrices(image_rows, rows):
    bands = band_products(image_rows)

    def taps(lines, first, last):
        parts = []
        for level, band in enumerate(bands):
            high, low = split_exact(np.pad(band, ((0, 0), (HALO, HALO)))[lines, first + HALO : last + HALO])
            scale = 1.0 / 16 ** (level + 1)
            parts.append(high * scale)
            if level >= 2:
                parts.append(low * scale)
        return np.concatenate(parts, axis=0)

    inner = np.arange(HALO, rows - HALO)
    edge = np.concatenate([np.arange(HALO), np.arange(rows - HALO, rows)])
    starts = [tile * rows for tile in (0, 1, image_rows // rows - 1)]
    return (
        taps(rows + inner, rows, 2 * rows).astype(jnp.bfloat16),
        np.stack([taps(start + edge, start - HALO, start + rows + HALO) for start in starts]).astype(jnp.bfloat16),
    )


def windows_of(columns):
    count = (columns - WINDOW) // STEP + 1
    assert (count - 1) * STEP + WINDOW == columns
    inside = [STEP * k + HALO for k in range(1, count)]
    return list(zip([0] + inside, inside + [columns]))


def column_matrices(columns):
    split = [split_exact(band) for band in band_products(columns)]
    parts = [high / 16 ** (level + 1) for level, (high, _) in enumerate(split)]
    parts += [low / 16 ** (level + 1) for level, (_, low) in enumerate(split) if level >= 2]
    made = np.zeros((len(windows_of(columns)), len(parts), WINDOW, WINDOW))
    for k, (first, last) in enumerate(windows_of(columns)):
        inputs, outputs = np.arange(STEP * k, STEP * k + WINDOW), np.arange(first, last)
        for j, part in enumerate(parts):
            made[k, j][np.ix_(inputs % WINDOW, outputs % WINDOW)] = part[np.ix_(outputs, inputs)].T
    return made.astype(jnp.bfloat16)


def filters(columns, rows, tiles):
    inner, edge = row_matrices(rows * tiles, rows)
    parts = [column_matrices(columns).reshape(-1, WINDOW)]
    for part in (inner, *edge):
        parts.append(np.pad(part, ((0, 0), (0, WINDOW - part.shape[1]))))
    return np.concatenate(parts, axis=0)


def dot(left, right):
    return jnp.dot(left, right, preferred_element_type=jnp.float32)


def luminance_of(colours):
    red, green, blue = (colours[channel].astype(jnp.float32) for channel in range(3))
    return (0.299 * red + 0.587 * green + 0.114 * blue).astype(jnp.bfloat16)


def combine(states):
    states = [[part.astype(jnp.float32) for part in state] for state in states]
    peak = functools.reduce(jnp.maximum, [state[0] for state in states])
    weights = [state[1] * jnp.exp(state[0] - peak) for state in states]
    total = sum(weights[1:], weights[0])
    inverse = 1.0 / total
    colours = []
    for channel in range(2, 5):
        terms = [weight * state[channel] for weight, state in zip(weights, states)]
        colours.append(sum(terms[1:], terms[0]) * inverse)
    return [peak, total] + colours


def fetch_kernel(planes_ref, stack_ref, core_ref, far_ref, arrived):
    depth, _, rows, _ = planes_ref.shape
    odd = lax.axis_index("tile") % 2
    copies = []
    for part, (start, count) in enumerate(((0, HALO), (rows - HALO, HALO), (HALO, rows - 2 * HALO))):
        at = pl.ds(start, count)
        copies.append(pltpu.make_async_copy(planes_ref.at[:, :, at], stack_ref.at[:, :, at], arrived.at[part]))
        copies[-1].start()
    copies[0].wait()
    copies[1].wait()
    tail, head = rows - HALO, 0
    for out, start in ((core_ref, jnp.where(odd == 0, tail, head)), (far_ref, jnp.where(odd == 0, head, tail))):
        at = pl.ds(pl.multiple_of(start, HALO), HALO)
        for plane in range(depth):
            out[plane] = luminance_of([stack_ref[plane, channel, at] for channel in range(3)])
    copies[2].wait()


def fetch(planes):
    depth, _, _, columns = planes.shape
    vmem = pl.BlockSpec(memory_space=pltpu.VMEM)
    shapes = [planes.shape] + [(depth, HALO, columns)] * 2
    return pl.pallas_call(
        fetch_kernel,
        out_shape=[jax.ShapeDtypeStruct(shape, jnp.bfloat16) for shape in shapes],
        in_specs=[pl.BlockSpec(memory_space=pl.ANY)],
        out_specs=[vmem] * 3,
        scratch_shapes=[pltpu.SemaphoreType.DMA((3,))],
        compiler_params=pltpu.CompilerParams(vmem_limit_bytes=50 * 2**20),
        cost_estimate=pl.CostEstimate(flops=2**32, bytes_accessed=64 * 2**20, transcendentals=0),
        name="fetch",
    )(planes)


def lane_below(limit, rows):
    return lax.broadcasted_iota(jnp.int32, (rows, LANES), 1) < limit


def filter_rows(row_ref, reach, window_of, depth, columns, high, low):
    count = row_ref.shape[0] // 6
    below = lane_below(LANES // 2, count)
    for plane in range(depth):
        here = pl.ds(plane * count, count)
        smooth = [dot(row_ref[:, :reach], window_of(plane, pl.ds(at, WINDOW))) for at in range(0, columns, WINDOW)]
        for level, parts in enumerate(((0,), (1,), (2, 3), (4, 5))):
            value = [sum(field[k * count : (k + 1) * count] for k in parts) for field in smooth]
            value = [half for field in value for half in (field[:, :LANES], field[:, LANES:])]
            for window in range(len(windows_of(columns))):
                first, mixed = divmod(STEP * window, LANES)
                for group in (first, first + 1):
                    line = value[group]
                    if mixed and group == first:
                        line = jnp.where(below, value[group + 2], line)
                    at = pl.ds(window * WINDOW + group % 2 * LANES, LANES)
                    top = line.astype(jnp.bfloat16)
                    high[level, here, at] = top
                    low[level, here, at] = (line - top.astype(jnp.float32)).astype(jnp.bfloat16)


def smooth_window(window, col_ref, high, low):
    at = pl.ds(window * WINDOW, WINDOW)
    made = []
    for level in range(LEVELS):
        top, rest = high[level, :, at], low[level, :, at]
        taps = [col_ref[pl.ds((window * 6 + k) * WINDOW, WINDOW)] for k in ((level,) if level < 2 else (level, level + 2))]
        value = dot(top, taps[0]) + dot(rest, taps[0])
        if level >= 2:
            value = value + dot(top, taps[1])
        made.append(value)
    return made


def scores(columns, luminance_at, gain_ref, col_ref, high, low):
    before = None
    ends = windows_of(columns)
    for window, (_, end) in enumerate(ends):
        after = smooth_window(window, col_ref, high, low)
        start = 0 if window == 0 else ends[window - 1][1] // LANES
        for group in range(start, end // LANES):
            at = pl.ds(group * LANES, LANES)
            half = slice(group % 2 * LANES, (group % 2 + 1) * LANES)
            approx = luminance_at(at).astype(jnp.float32)
            approx = approx.reshape(-1, LANES)
            score = jnp.zeros(approx.shape, jnp.float32)
            border = 0 if window == 0 else ends[window - 1][1] - group * LANES
            for level in range(LEVELS):
                smoother = after[level][:, half]
                if border > 0:
                    smoother = jnp.where(lane_below(border, smoother.shape[0]), before[level][:, half], smoother)
                detail = approx - smoother
                score = score + gain_ref[level] * detail * detail
                approx = smoother
            yield at, score
        before = after


def state_of(score, colours):
    peak = jnp.max(score, axis=0).astype(jnp.bfloat16)
    weight = jnp.exp(score - peak.astype(jnp.float32)[None])
    total = jnp.sum(weight, axis=0)
    inverse = 1.0 / total
    means = [jnp.sum(weight * colour.astype(jnp.float32), axis=0) * inverse for colour in colours]
    return [peak, total.astype(jnp.bfloat16)] + [mean.astype(jnp.bfloat16) for mean in means]


def inner_kernel(
    gain_ref, planes_ref, taps_ref, lum_ref, row_ref, col_ref, state_ref, spread_ref, gain, inner, high, low, arrived
):
    depth, _, rows, columns = planes_ref.shape
    bands, _, share, _ = state_ref.shape
    count = rows - 2 * HALO
    tile, tiles = lax.axis_index("tile"), lax.axis_size("tile")
    tile_case = jnp.where(tile == 0, 0, jnp.where(tile == tiles - 1, 2, 1))
    lines, first = inner.shape[0], col_ref.shape[0]
    edge = pl.multiple_of(first + lines + tile_case * row_ref.shape[0], LANES)
    copies = []
    copies.append(pltpu.make_async_copy(gain_ref, gain, arrived.at[0]))
    copies[0].start()
    for start, target in ((first, inner), (0, col_ref), (edge, row_ref)):
        source = taps_ref.at[pl.ds(start, target.shape[0])]
        copies.append(pltpu.make_async_copy(source, target, arrived.at[len(copies)]))
        copies[-1].start()
    for plane in range(depth):
        lum_ref[plane] = luminance_of([planes_ref[plane, channel] for channel in range(3)])
    copies[1].wait()
    filter_rows(inner, rows, lambda plane, at: lum_ref[plane, :, at], depth, columns, high, low)
    copies[0].wait()
    for level in range(LEVELS):
        spread_ref[level] = jnp.full((1, LANES), gain[level], jnp.float32)
    copies[2].wait()
    inside = pl.ds(HALO, count)
    for at, score in scores(columns, lambda at: lum_ref[:, inside, at], gain, col_ref, high, low):
        colours = [planes_ref[:, channel, inside, at] for channel in range(3)]
        for k, part in enumerate(state_of(score.reshape(depth, count, LANES), colours)):
            state_ref[:, k, :, at] = part.reshape(bands, share, LANES)
    copies[3].wait()


def inner_state(planes, level_gain, groups, tiles):
    depth, channels, rows, columns = planes.shape
    count, share = rows - 2 * HALO, rows // groups
    taps = jnp.asarray(filters(columns, rows, tiles))
    inner_lines, edge_lines = 6 * count, 12 * HALO
    vmem = pl.BlockSpec(memory_space=pltpu.VMEM)
    window_lines = taps.shape[0] - inner_lines - 3 * edge_lines
    shapes = [(depth, rows, columns), (edge_lines, WINDOW), (window_lines, WINDOW), (count // share, 5, share, columns)]
    wide = len(windows_of(columns)) * WINDOW
    return pl.pallas_call(
        inner_kernel,
        out_shape=[jax.ShapeDtypeStruct(shape, jnp.bfloat16) for shape in shapes]
        + [jax.ShapeDtypeStruct((LEVELS, 1, LANES), jnp.float32)],
        in_specs=[pl.BlockSpec(memory_space=pl.ANY), vmem, pl.BlockSpec(memory_space=pl.ANY)],
        out_specs=[vmem] * (len(shapes) + 1),
        scratch_shapes=[
            pltpu.SMEM((LEVELS,), jnp.float32),
            pltpu.VMEM((inner_lines, WINDOW), jnp.bfloat16),
            pltpu.VMEM((LEVELS, depth * count, wide), jnp.bfloat16),
            pltpu.VMEM((LEVELS, depth * count, wide), jnp.bfloat16),
            pltpu.SemaphoreType.DMA((4,)),
        ],
        compiler_params=pltpu.CompilerParams(vmem_limit_bytes=43 * 2**20),
        cost_estimate=pl.CostEstimate(flops=2**30, bytes_accessed=10 * 2**20, transcendentals=0),
        name="inner_state",
    )(level_gain, planes, taps)


def edge_state_kernel(slow, planes_ref, lum_ref, row_ref, col_ref, inner_ref, gain_ref, core_ref, far_ref, *refs):
    *outs, halo, high, low, held = refs
    depth, _, rows, columns = planes_ref.shape
    groups, _, share, _ = held.shape
    fast = groups // slow
    split = outs[0].shape[-1]
    odd = lax.axis_index("tile") % 2

    def place_halo(above_ref, below_ref):
        halo[0] = above_ref[...]
        halo[1] = below_ref[...]

    pl.when(odd == 0)(lambda: place_halo(far_ref, core_ref))
    pl.when(odd == 1)(lambda: place_halo(core_ref, far_ref))

    def window_of(plane, at):
        return jnp.concatenate([halo[0, plane, :, at], lum_ref[plane, :, at], halo[1, plane, :, at]], axis=0)

    def edges_of(ref, *index):
        return jnp.concatenate([ref[index[:-1] + (pl.ds(start, HALO), index[-1])] for start in (0, rows - HALO)], axis=-2)

    filter_rows(row_ref, rows + 2 * HALO, window_of, depth, columns, high, low)
    side = HALO // share
    held[side : groups - side] = inner_ref[...]
    for at, score in scores(columns, lambda at: edges_of(lum_ref, slice(None), at), gain_ref, col_ref, high, low):
        colours = [edges_of(planes_ref, slice(None), channel, at) for channel in range(3)]
        for k, part in enumerate(state_of(score.reshape(depth, 2 * HALO, LANES), colours)):
            held[:side, k, :, at] = part[:HALO].reshape(side, share, LANES)
            held[groups - side :, k, :, at] = part[HALO:].reshape(side, share, LANES)

    group = lax.axis_index("gz")
    mine_slow, mine_fast = group // fast, group % fast
    for other in range(fast):
        for place in range(slow):
            outs[other][place] = held[place * fast + (mine_fast ^ other), :, :, :split]
    for other in range(slow):
        for place in range(fast):
            outs[fast + other][place] = held[(mine_slow ^ other) * fast + place, :, :, split:]


def edge_state(planes, inner, core, far, slow, groups, split):
    depth, _, rows, columns = planes.shape
    fast, share = groups // slow, rows // groups
    vmem = pl.BlockSpec(memory_space=pltpu.VMEM)
    wide = len(windows_of(columns)) * WINDOW
    shapes = [(slow, 5, share, split)] * fast + [(fast, 5, share, columns - split)] * slow
    return pl.pallas_call(
        functools.partial(edge_state_kernel, slow),
        out_shape=[jax.ShapeDtypeStruct(shape, jnp.bfloat16) for shape in shapes],
        in_specs=[vmem] * 8,
        out_specs=[vmem] * len(shapes),
        scratch_shapes=[
            pltpu.VMEM((2, depth, HALO, columns), jnp.bfloat16),
            pltpu.VMEM((LEVELS, 2 * depth * HALO, wide), jnp.bfloat16),
            pltpu.VMEM((LEVELS, 2 * depth * HALO, wide), jnp.bfloat16),
            pltpu.VMEM((groups, 5, share, columns), jnp.bfloat16),
        ],
        compiler_params=pltpu.CompilerParams(vmem_limit_bytes=40 * 2**20),
        name="edge_state",
    )(planes, *inner, core, far)


def merge_kernel(count, pick, *refs):
    states, outs, held = refs[:count], refs[count:-1], refs[-1]
    for place in range(held.shape[0]):
        for k, part in enumerate(combine([[state[place, k] for k in range(5)] for state in states])):
            held[place, k] = part.astype(jnp.bfloat16)
    place = pick(lax.axis_index("gz"))
    for other, out in enumerate(outs):
        out[...] = held[place ^ other]


def merge(states, pick):
    bands, _, share, columns = states[0].shape
    return pl.pallas_call(
        functools.partial(merge_kernel, len(states), pick),
        out_shape=[jax.ShapeDtypeStruct((5, share, columns), jnp.bfloat16)] * bands,
        scratch_shapes=[pltpu.VMEM(states[0].shape, jnp.bfloat16)],
        compiler_params=pltpu.CompilerParams(vmem_limit_bytes=16 * 2**20),
        name="merge",
    )(*states)


def join_kernel(counts, *refs):
    *refs, out_ref = refs
    start = 0
    for count in counts:
        states, refs = refs[:count], refs[count:]
        width = states[0].shape[-1]
        merged = combine([[state[k] for k in range(5)] for state in states])
        for channel in range(3):
            out_ref[channel, :, start : start + width] = merged[2 + channel].astype(jnp.bfloat16)
        start += width


def join(*parts):
    share = parts[0][0].shape[1]
    columns = sum(part[0].shape[2] for part in parts)
    return pl.pallas_call(
        functools.partial(join_kernel, [len(part) for part in parts]),
        out_shape=jax.ShapeDtypeStruct((3, share, columns), jnp.bfloat16),
        compiler_params=pltpu.CompilerParams(vmem_limit_bytes=16 * 2**20),
        name="join",
    )(*[state for part in parts for state in part])


def swap(states, groups, step, order):
    moved = [lax.ppermute(states[k], "gz", [(i, i ^ (k * step)) for i in range(groups)]) for k in order]
    return [states[0]] + moved


def per_device(planes, level_gain):
    columns = planes.shape[3]
    tiles = lax.axis_size("tile")
    groups = lax.axis_size("gz")
    slow = min(4, groups)
    fast = groups // slow
    split = 5 * columns // 8
    stack, to_core, to_far = fetch(planes)
    core = lax.ppermute(to_core, "tile", [(i, i ^ 1) for i in range(tiles)])
    between = range(1, tiles - 1, 2)
    far = lax.ppermute(to_far, "tile", [(i, i + 1) for i in between] + [(i + 1, i) for i in between])
    inner = inner_state(stack, level_gain, groups, tiles)
    states = edge_state(stack, inner, core, far, slow, groups, split)
    near = range(1, fast)
    first = swap(states[:fast], groups, 1, near)
    second = swap(states[fast:], groups, fast, FAR_FIRST)
    first = swap(merge(first, lambda group: group // fast), groups, fast, range(1, slow))
    second = swap(merge(second, lambda group: group % fast), groups, 1, near)
    return join(first, second)


def solution(mesh):
    return jax.shard_map(
        per_device,
        mesh=mesh,
        in_specs=(P("gz", None, "tile", None), P()),
        out_specs=P(None, ("tile", "gz"), None),
        check_vma=False,
    )
```

```python
import functools

import jax
import jax.numpy as jnp
import numpy as np
from jax import lax
from jax.experimental import pallas as pl
from jax.experimental.pallas import tpu as pltpu
from jax.sharding import PartitionSpec as P

LEVELS = 4
TAPS = (1, 4, 6, 4, 1)
HALO = 32
LANES = 128
WINDOW = 256
STEP = 192
FAR_FIRST = (3, 1, 2)


def band_products(count):
    made = []
    whole = np.eye(count)
    for level in range(LEVELS):
        step = sum(tap * np.eye(count, k=(place - 2) * 2**level) for place, tap in enumerate(TAPS))
        whole = step @ whole
        made.append(whole)
    return made


def split_exact(matrix):
    high = matrix.astype(jnp.bfloat16).astype(matrix.dtype)
    return high, matrix - high


def row_matrices(image_rows, rows):
    bands = band_products(image_rows)

    def taps(lines, first, last):
        parts = []
        for level, band in enumerate(bands):
            high, low = split_exact(np.pad(band, ((0, 0), (HALO, HALO)))[lines, first + HALO : last + HALO])
            scale = 1.0 / 16 ** (level + 1)
            parts.append(high * scale)
            if level >= 2:
                parts.append(low * scale)
        return np.concatenate(parts, axis=0)

    inner = np.arange(HALO, rows - HALO)
    edge = np.concatenate([np.arange(HALO), np.arange(rows - HALO, rows)])
    starts = [tile * rows for tile in (0, 1, image_rows // rows - 1)]
    return (
        taps(rows + inner, rows, 2 * rows).astype(jnp.bfloat16),
        np.stack([taps(start + edge, start - HALO, start + rows + HALO) for start in starts]).astype(jnp.bfloat16),
    )


def windows_of(columns):
    count = (columns - WINDOW) // STEP + 1
    assert (count - 1) * STEP + WINDOW == columns
    inside = [STEP * k + HALO for k in range(1, count)]
    return list(zip([0] + inside, inside + [columns]))


def column_matrices(columns):
    split = [split_exact(band) for band in band_products(columns)]
    parts = [high / 16 ** (level + 1) for level, (high, _) in enumerate(split)]
    parts += [low / 16 ** (level + 1) for level, (_, low) in enumerate(split) if level >= 2]
    made = np.zeros((len(windows_of(columns)), len(parts), WINDOW, WINDOW))
    for k, (first, last) in enumerate(windows_of(columns)):
        inputs, outputs = np.arange(STEP * k, STEP * k + WINDOW), np.arange(first, last)
        for j, part in enumerate(parts):
            made[k, j][np.ix_(inputs % WINDOW, outputs % WINDOW)] = part[np.ix_(outputs, inputs)].T
    return made.astype(jnp.bfloat16)


def filters(columns, rows, tiles):
    inner, edge = row_matrices(rows * tiles, rows)
    parts = [column_matrices(columns).reshape(-1, WINDOW)]
    for part in (inner, *edge):
        parts.append(np.pad(part, ((0, 0), (0, WINDOW - part.shape[1]))))
    return np.concatenate(parts, axis=0)


def dot(left, right):
    return jnp.dot(left, right, preferred_element_type=jnp.float32)


def luminance_of(colours):
    red, green, blue = (colours[channel].astype(jnp.float32) for channel in range(3))
    return (0.299 * red + 0.587 * green + 0.114 * blue).astype(jnp.bfloat16)


def combine(states):
    states = [[part.astype(jnp.float32) for part in state] for state in states]
    peak = functools.reduce(jnp.maximum, [state[0] for state in states])
    weights = [state[1] * jnp.exp(state[0] - peak) for state in states]
    total = sum(weights[1:], weights[0])
    inverse = 1.0 / total
    colours = []
    for channel in range(2, 5):
        terms = [weight * state[channel] for weight, state in zip(weights, states)]
        colours.append(sum(terms[1:], terms[0]) * inverse)
    return [peak, total] + colours


def fetch_kernel(planes_ref, stack_ref, core_ref, far_ref, arrived):
    depth, _, rows, _ = planes_ref.shape
    odd = lax.axis_index("tile") % 2
    copies = []
    for part, (start, count) in enumerate(((0, HALO), (rows - HALO, HALO), (HALO, rows - 2 * HALO))):
        at = pl.ds(start, count)
        copies.append(pltpu.make_async_copy(planes_ref.at[:, :, at], stack_ref.at[:, :, at], arrived.at[part]))
        copies[-1].start()
    copies[0].wait()
    copies[1].wait()
    tail, head = rows - HALO, 0
    for out, start in ((core_ref, jnp.where(odd == 0, tail, head)), (far_ref, jnp.where(odd == 0, head, tail))):
        at = pl.ds(pl.multiple_of(start, HALO), HALO)
        for plane in range(depth):
            out[plane] = luminance_of([stack_ref[plane, channel, at] for channel in range(3)])
    copies[2].wait()


def fetch(planes):
    depth, _, _, columns = planes.shape
    vmem = pl.BlockSpec(memory_space=pltpu.VMEM)
    shapes = [planes.shape] + [(depth, HALO, columns)] * 2
    return pl.pallas_call(
        fetch_kernel,
        out_shape=[jax.ShapeDtypeStruct(shape, jnp.bfloat16) for shape in shapes],
        in_specs=[pl.BlockSpec(memory_space=pl.ANY)],
        out_specs=[vmem] * 3,
        scratch_shapes=[pltpu.SemaphoreType.DMA((3,))],
        compiler_params=pltpu.CompilerParams(vmem_limit_bytes=50 * 2**20),
        cost_estimate=pl.CostEstimate(flops=2**32, bytes_accessed=64 * 2**20, transcendentals=0),
        name="fetch",
    )(planes)


def lane_below(limit, rows):
    return lax.broadcasted_iota(jnp.int32, (rows, LANES), 1) < limit


def filter_rows(row_ref, reach, window_of, depth, columns, high, low):
    count = row_ref.shape[0] // 6
    below = lane_below(LANES // 2, count)
    for plane in range(depth):
        here = pl.ds(plane * count, count)
        smooth = [dot(row_ref[:, :reach], window_of(plane, pl.ds(at, WINDOW))) for at in range(0, columns, WINDOW)]
        for level, parts in enumerate(((0,), (1,), (2, 3), (4, 5))):
            value = [sum(field[k * count : (k + 1) * count] for k in parts) for field in smooth]
            value = [half for field in value for half in (field[:, :LANES], field[:, LANES:])]
            for window in range(len(windows_of(columns))):
                first, mixed = divmod(STEP * window, LANES)
                for group in (first, first + 1):
                    line = value[group]
                    if mixed and group == first:
                        line = jnp.where(below, value[group + 2], line)
                    at = pl.ds(window * WINDOW + group % 2 * LANES, LANES)
                    top = line.astype(jnp.bfloat16)
                    high[level, here, at] = top
                    low[level, here, at] = (line - top.astype(jnp.float32)).astype(jnp.bfloat16)


def smooth_window(window, col_ref, high, low):
    at = pl.ds(window * WINDOW, WINDOW)
    made = []
    for level in range(LEVELS):
        top, rest = high[level, :, at], low[level, :, at]
        taps = [col_ref[pl.ds((window * 6 + k) * WINDOW, WINDOW)] for k in ((level,) if level < 2 else (level, level + 2))]
        lines, factors = [top, rest] + [top] * (level >= 2), [taps[0]] + taps
        value = dot(jnp.concatenate(lines, axis=1), jnp.concatenate(factors, axis=0))
        made.append(value)
    return made


def scores(columns, luminance_at, gain_ref, col_ref, high, low):
    before = None
    ends = windows_of(columns)
    for window, (_, end) in enumerate(ends):
        after = smooth_window(window, col_ref, high, low)
        start = 0 if window == 0 else ends[window - 1][1] // LANES
        for group in range(start, end // LANES):
            at = pl.ds(group * LANES, LANES)
            half = slice(group % 2 * LANES, (group % 2 + 1) * LANES)
            approx = luminance_at(at).astype(jnp.float32)
            approx = approx.reshape(-1, LANES)
            score = jnp.zeros(approx.shape, jnp.float32)
            border = 0 if window == 0 else ends[window - 1][1] - group * LANES
            for level in range(LEVELS):
                smoother = after[level][:, half]
                if border > 0:
                    smoother = jnp.where(lane_below(border, smoother.shape[0]), before[level][:, half], smoother)
                detail = approx - smoother
                score = score + gain_ref[level] * detail * detail
                approx = smoother
            yield at, score
        before = after


def state_of(score, colours):
    peak = jnp.max(score, axis=0).astype(jnp.bfloat16)
    weight = jnp.exp(score - peak.astype(jnp.float32)[None])
    total = jnp.sum(weight, axis=0)
    inverse = 1.0 / total
    means = [jnp.sum(weight * colour.astype(jnp.float32), axis=0) * inverse for colour in colours]
    return [peak, total.astype(jnp.bfloat16)] + [mean.astype(jnp.bfloat16) for mean in means]


def inner_kernel(
    gain_ref, planes_ref, taps_ref, lum_ref, row_ref, col_ref, state_ref, spread_ref, gain, inner, high, low, arrived
):
    depth, _, rows, columns = planes_ref.shape
    bands, _, share, _ = state_ref.shape
    count = rows - 2 * HALO
    tile, tiles = lax.axis_index("tile"), lax.axis_size("tile")
    tile_case = jnp.where(tile == 0, 0, jnp.where(tile == tiles - 1, 2, 1))
    lines, first = inner.shape[0], col_ref.shape[0]
    edge = pl.multiple_of(first + lines + tile_case * row_ref.shape[0], LANES)
    copies = []
    copies.append(pltpu.make_async_copy(gain_ref, gain, arrived.at[0]))
    copies[0].start()
    for start, target in ((first, inner), (0, col_ref), (edge, row_ref)):
        source = taps_ref.at[pl.ds(start, target.shape[0])]
        copies.append(pltpu.make_async_copy(source, target, arrived.at[len(copies)]))
        copies[-1].start()
    for plane in range(depth):
        lum_ref[plane] = luminance_of([planes_ref[plane, channel] for channel in range(3)])
    copies[1].wait()
    filter_rows(inner, rows, lambda plane, at: lum_ref[plane, :, at], depth, columns, high, low)
    copies[0].wait()
    for level in range(LEVELS):
        spread_ref[level] = jnp.full((1, LANES), gain[level], jnp.float32)
    copies[2].wait()
    inside = pl.ds(HALO, count)
    for at, score in scores(columns, lambda at: lum_ref[:, inside, at], gain, col_ref, high, low):
        colours = [planes_ref[:, channel, inside, at] for channel in range(3)]
        for k, part in enumerate(state_of(score.reshape(depth, count, LANES), colours)):
            state_ref[:, k, :, at] = part.reshape(bands, share, LANES)
    copies[3].wait()


def inner_state(planes, level_gain, groups, tiles):
    depth, channels, rows, columns = planes.shape
    count, share = rows - 2 * HALO, rows // groups
    taps = jnp.asarray(filters(columns, rows, tiles))
    inner_lines, edge_lines = 6 * count, 12 * HALO
    vmem = pl.BlockSpec(memory_space=pltpu.VMEM)
    window_lines = taps.shape[0] - inner_lines - 3 * edge_lines
    shapes = [(depth, rows, columns), (edge_lines, WINDOW), (window_lines, WINDOW), (count // share, 5, share, columns)]
    wide = len(windows_of(columns)) * WINDOW
    return pl.pallas_call(
        inner_kernel,
        out_shape=[jax.ShapeDtypeStruct(shape, jnp.bfloat16) for shape in shapes]
        + [jax.ShapeDtypeStruct((LEVELS, 1, LANES), jnp.float32)],
        in_specs=[pl.BlockSpec(memory_space=pl.ANY), vmem, pl.BlockSpec(memory_space=pl.ANY)],
        out_specs=[vmem] * (len(shapes) + 1),
        scratch_shapes=[
            pltpu.SMEM((LEVELS,), jnp.float32),
            pltpu.VMEM((inner_lines, WINDOW), jnp.bfloat16),
            pltpu.VMEM((LEVELS, depth * count, wide), jnp.bfloat16),
            pltpu.VMEM((LEVELS, depth * count, wide), jnp.bfloat16),
            pltpu.SemaphoreType.DMA((4,)),
        ],
        compiler_params=pltpu.CompilerParams(vmem_limit_bytes=43 * 2**20),
        cost_estimate=pl.CostEstimate(flops=2**30, bytes_accessed=10 * 2**20, transcendentals=0),
        name="inner_state",
    )(level_gain, planes, taps)


def edge_state_kernel(slow, planes_ref, lum_ref, row_ref, col_ref, inner_ref, gain_ref, core_ref, far_ref, *refs):
    *outs, halo, high, low, held = refs
    depth, _, rows, columns = planes_ref.shape
    groups, _, share, _ = held.shape
    fast = groups // slow
    split = outs[0].shape[-1]
    odd = lax.axis_index("tile") % 2

    def place_halo(above_ref, below_ref):
        halo[0] = above_ref[...]
        halo[1] = below_ref[...]

    pl.when(odd == 0)(lambda: place_halo(far_ref, core_ref))
    pl.when(odd == 1)(lambda: place_halo(core_ref, far_ref))

    def window_of(plane, at):
        return jnp.concatenate([halo[0, plane, :, at], lum_ref[plane, :, at], halo[1, plane, :, at]], axis=0)

    def edges_of(ref, *index):
        return jnp.concatenate([ref[index[:-1] + (pl.ds(start, HALO), index[-1])] for start in (0, rows - HALO)], axis=-2)

    filter_rows(row_ref, rows + 2 * HALO, window_of, depth, columns, high, low)
    side = HALO // share
    held[side : groups - side] = inner_ref[...]
    for at, score in scores(columns, lambda at: edges_of(lum_ref, slice(None), at), gain_ref, col_ref, high, low):
        colours = [edges_of(planes_ref, slice(None), channel, at) for channel in range(3)]
        for k, part in enumerate(state_of(score.reshape(depth, 2 * HALO, LANES), colours)):
            held[:side, k, :, at] = part[:HALO].reshape(side, share, LANES)
            held[groups - side :, k, :, at] = part[HALO:].reshape(side, share, LANES)

    group = lax.axis_index("gz")
    mine_slow, mine_fast = group // fast, group % fast
    for other in range(fast):
        for place in range(slow):
            outs[other][place] = held[place * fast + (mine_fast ^ other), :, :, :split]
    for other in range(slow):
        for place in range(fast):
            outs[fast + other][place] = held[(mine_slow ^ other) * fast + place, :, :, split:]


def edge_state(planes, inner, core, far, slow, groups, split):
    depth, _, rows, columns = planes.shape
    fast, share = groups // slow, rows // groups
    vmem = pl.BlockSpec(memory_space=pltpu.VMEM)
    wide = len(windows_of(columns)) * WINDOW
    shapes = [(slow, 5, share, split)] * fast + [(fast, 5, share, columns - split)] * slow
    return pl.pallas_call(
        functools.partial(edge_state_kernel, slow),
        out_shape=[jax.ShapeDtypeStruct(shape, jnp.bfloat16) for shape in shapes],
        in_specs=[vmem] * 8,
        out_specs=[vmem] * len(shapes),
        scratch_shapes=[
            pltpu.VMEM((2, depth, HALO, columns), jnp.bfloat16),
            pltpu.VMEM((LEVELS, 2 * depth * HALO, wide), jnp.bfloat16),
            pltpu.VMEM((LEVELS, 2 * depth * HALO, wide), jnp.bfloat16),
            pltpu.VMEM((groups, 5, share, columns), jnp.bfloat16),
        ],
        compiler_params=pltpu.CompilerParams(vmem_limit_bytes=40 * 2**20),
        name="edge_state",
    )(planes, *inner, core, far)


def merge_kernel(count, pick, *refs):
    states, outs, held = refs[:count], refs[count:-1], refs[-1]
    for place in range(held.shape[0]):
        for k, part in enumerate(combine([[state[place, k] for k in range(5)] for state in states])):
            held[place, k] = part.astype(jnp.bfloat16)
    place = pick(lax.axis_index("gz"))
    for other, out in enumerate(outs):
        out[...] = held[place ^ other]


def merge(states, pick):
    bands, _, share, columns = states[0].shape
    return pl.pallas_call(
        functools.partial(merge_kernel, len(states), pick),
        out_shape=[jax.ShapeDtypeStruct((5, share, columns), jnp.bfloat16)] * bands,
        scratch_shapes=[pltpu.VMEM(states[0].shape, jnp.bfloat16)],
        compiler_params=pltpu.CompilerParams(vmem_limit_bytes=16 * 2**20),
        name="merge",
    )(*states)


def join_kernel(counts, *refs):
    *refs, out_ref = refs
    start = 0
    for count in counts:
        states, refs = refs[:count], refs[count:]
        width = states[0].shape[-1]
        merged = combine([[state[k] for k in range(5)] for state in states])
        for channel in range(3):
            out_ref[channel, :, start : start + width] = merged[2 + channel].astype(jnp.bfloat16)
        start += width


def join(*parts):
    share = parts[0][0].shape[1]
    columns = sum(part[0].shape[2] for part in parts)
    return pl.pallas_call(
        functools.partial(join_kernel, [len(part) for part in parts]),
        out_shape=jax.ShapeDtypeStruct((3, share, columns), jnp.bfloat16),
        compiler_params=pltpu.CompilerParams(vmem_limit_bytes=16 * 2**20),
        name="join",
    )(*[state for part in parts for state in part])


def swap(states, groups, step, order):
    moved = [lax.ppermute(states[k], "gz", [(i, i ^ (k * step)) for i in range(groups)]) for k in order]
    return [states[0]] + moved


def per_device(planes, level_gain):
    columns = planes.shape[3]
    tiles = lax.axis_size("tile")
    groups = lax.axis_size("gz")
    slow = min(4, groups)
    fast = groups // slow
    split = 5 * columns // 8
    stack, to_core, to_far = fetch(planes)
    core = lax.ppermute(to_core, "tile", [(i, i ^ 1) for i in range(tiles)])
    between = range(1, tiles - 1, 2)
    far = lax.ppermute(to_far, "tile", [(i, i + 1) for i in between] + [(i + 1, i) for i in between])
    inner = inner_state(stack, level_gain, groups, tiles)
    states = edge_state(stack, inner, core, far, slow, groups, split)
    near = range(1, fast)
    first = swap(states[:fast], groups, 1, near)
    second = swap(states[fast:], groups, fast, FAR_FIRST)
    first = swap(merge(first, lambda group: group // fast), groups, fast, range(1, slow))
    second = swap(merge(second, lambda group: group % fast), groups, 1, near)
    return join(first, second)


def solution(mesh):
    return jax.shard_map(
        per_device,
        mesh=mesh,
        in_specs=(P("gz", None, "tile", None), P()),
        out_specs=P(None, ("tile", "gz"), None),
        check_vma=False,
    )
```

```python
import functools

import jax
import jax.numpy as jnp
import numpy as np
from jax import lax
from jax.experimental import pallas as pl
from jax.experimental.pallas import tpu as pltpu
from jax.sharding import PartitionSpec as P

LEVELS = 4
TAPS = (1, 4, 6, 4, 1)
HALO = 32
LANES = 128
WINDOW = 256
STEP = 192
FAR_FIRST = (3, 2, 1)


def band_products(count):
    made = []
    whole = np.eye(count)
    for level in range(LEVELS):
        step = sum(tap * np.eye(count, k=(place - 2) * 2**level) for place, tap in enumerate(TAPS))
        whole = step @ whole
        made.append(whole)
    return made


def split_exact(matrix):
    high = matrix.astype(jnp.bfloat16).astype(matrix.dtype)
    return high, matrix - high


def row_matrices(image_rows, rows):
    bands = band_products(image_rows)

    def taps(lines, first, last):
        parts = []
        for level, band in enumerate(bands):
            high, low = split_exact(np.pad(band, ((0, 0), (HALO, HALO)))[lines, first + HALO : last + HALO])
            scale = 1.0 / 16 ** (level + 1)
            parts.append(high * scale)
            if level >= 2:
                parts.append(low * scale)
        return np.concatenate(parts, axis=0)

    inner = np.arange(HALO, rows - HALO)
    edge = np.concatenate([np.arange(HALO), np.arange(rows - HALO, rows)])
    starts = [tile * rows for tile in (0, 1, image_rows // rows - 1)]
    return (
        taps(rows + inner, rows, 2 * rows).astype(jnp.bfloat16),
        np.stack([taps(start + edge, start - HALO, start + rows + HALO) for start in starts]).astype(jnp.bfloat16),
    )


def windows_of(columns):
    count = (columns - WINDOW) // STEP + 1
    assert (count - 1) * STEP + WINDOW == columns
    inside = [STEP * k + HALO for k in range(1, count)]
    return list(zip([0] + inside, inside + [columns]))


def column_matrices(columns):
    split = [split_exact(band) for band in band_products(columns)]
    parts = [high / 16 ** (level + 1) for level, (high, _) in enumerate(split)]
    parts += [low / 16 ** (level + 1) for level, (_, low) in enumerate(split) if level >= 2]
    made = np.zeros((len(windows_of(columns)), len(parts), WINDOW, WINDOW))
    for k, (first, last) in enumerate(windows_of(columns)):
        inputs, outputs = np.arange(STEP * k, STEP * k + WINDOW), np.arange(first, last)
        for j, part in enumerate(parts):
            made[k, j][np.ix_(inputs % WINDOW, outputs % WINDOW)] = part[np.ix_(outputs, inputs)].T
    return made.astype(jnp.bfloat16)


def filters(columns, rows, tiles):
    inner, edge = row_matrices(rows * tiles, rows)
    parts = [column_matrices(columns).reshape(-1, WINDOW)]
    for part in (inner, *edge):
        parts.append(np.pad(part, ((0, 0), (0, WINDOW - part.shape[1]))))
    return np.concatenate(parts, axis=0)


def dot(left, right):
    return jnp.dot(left, right, preferred_element_type=jnp.float32)


def luminance_of(colours):
    red, green, blue = (colours[channel].astype(jnp.float32) for channel in range(3))
    return (0.299 * red + 0.587 * green + 0.114 * blue).astype(jnp.bfloat16)


def combine(states):
    states = [[part.astype(jnp.float32) for part in state] for state in states]
    peak = functools.reduce(jnp.maximum, [state[0] for state in states])
    weights = [state[1] * jnp.exp(state[0] - peak) for state in states]
    total = sum(weights[1:], weights[0])
    inverse = 1.0 / total
    colours = []
    for channel in range(2, 5):
        terms = [weight * state[channel] for weight, state in zip(weights, states)]
        colours.append(sum(terms[1:], terms[0]) * inverse)
    return [peak, total] + colours


def fetch_kernel(planes_ref, stack_ref, core_ref, far_ref, arrived):
    depth, _, rows, _ = planes_ref.shape
    odd = lax.axis_index("tile") % 2
    copies = []
    for part, (start, count) in enumerate(((0, HALO), (rows - HALO, HALO), (HALO, rows - 2 * HALO))):
        at = pl.ds(start, count)
        copies.append(pltpu.make_async_copy(planes_ref.at[:, :, at], stack_ref.at[:, :, at], arrived.at[part]))
        copies[-1].start()
    copies[0].wait()
    copies[1].wait()
    tail, head = rows - HALO, 0
    for out, start in ((core_ref, jnp.where(odd == 0, tail, head)), (far_ref, jnp.where(odd == 0, head, tail))):
        at = pl.ds(pl.multiple_of(start, HALO), HALO)
        for plane in range(depth):
            out[plane] = luminance_of([stack_ref[plane, channel, at] for channel in range(3)])
    copies[2].wait()


def fetch(planes):
    depth, _, _, columns = planes.shape
    vmem = pl.BlockSpec(memory_space=pltpu.VMEM)
    shapes = [planes.shape] + [(depth, HALO, columns)] * 2
    return pl.pallas_call(
        fetch_kernel,
        out_shape=[jax.ShapeDtypeStruct(shape, jnp.bfloat16) for shape in shapes],
        in_specs=[pl.BlockSpec(memory_space=pl.ANY)],
        out_specs=[vmem] * 3,
        scratch_shapes=[pltpu.SemaphoreType.DMA((3,))],
        compiler_params=pltpu.CompilerParams(vmem_limit_bytes=50 * 2**20),
        cost_estimate=pl.CostEstimate(flops=2**32, bytes_accessed=64 * 2**20, transcendentals=0),
        name="fetch",
    )(planes)


def lane_below(limit, rows):
    return lax.broadcasted_iota(jnp.int32, (rows, LANES), 1) < limit


def filter_rows(row_ref, reach, window_of, depth, columns, high, low):
    count = row_ref.shape[0] // 6
    below = lane_below(LANES // 2, count)
    for plane in range(depth):
        here = pl.ds(plane * count, count)
        smooth = [dot(row_ref[:, :reach], window_of(plane, pl.ds(at, WINDOW))) for at in range(0, columns, WINDOW)]
        for level, parts in enumerate(((0,), (1,), (2, 3), (4, 5))):
            value = [sum(field[k * count : (k + 1) * count] for k in parts) for field in smooth]
            value = [half for field in value for half in (field[:, :LANES], field[:, LANES:])]
            for window in range(len(windows_of(columns))):
                first, mixed = divmod(STEP * window, LANES)
                for group in (first, first + 1):
                    line = value[group]
                    if mixed and group == first:
                        line = jnp.where(below, value[group + 2], line)
                    at = pl.ds(window * WINDOW + group % 2 * LANES, LANES)
                    top = line.astype(jnp.bfloat16)
                    high[level, here, at] = top
                    low[level, here, at] = (line - top.astype(jnp.float32)).astype(jnp.bfloat16)


def smooth_window(window, col_ref, high, low):
    at = pl.ds(window * WINDOW, WINDOW)
    made = []
    for level in range(LEVELS):
        top, rest = high[level, :, at], low[level, :, at]
        taps = [col_ref[pl.ds((window * 6 + k) * WINDOW, WINDOW)] for k in ((level,) if level < 2 else (level, level + 2))]
        lines, factors = [top, rest] + [top] * (level >= 2), [taps[0]] + taps
        value = dot(jnp.concatenate(lines, axis=1), jnp.concatenate(factors, axis=0))
        made.append(value)
    return made


def scores(columns, luminance_at, gain_ref, col_ref, high, low):
    before = None
    ends = windows_of(columns)
    for window, (_, end) in enumerate(ends):
        after = smooth_window(window, col_ref, high, low)
        start = 0 if window == 0 else ends[window - 1][1] // LANES
        for group in range(start, end // LANES):
            at = pl.ds(group * LANES, LANES)
            half = slice(group % 2 * LANES, (group % 2 + 1) * LANES)
            approx = luminance_at(at).astype(jnp.float32)
            approx = approx.reshape(-1, LANES)
            score = jnp.zeros(approx.shape, jnp.float32)
            border = 0 if window == 0 else ends[window - 1][1] - group * LANES
            for level in range(LEVELS):
                smoother = after[level][:, half]
                if border > 0:
                    smoother = jnp.where(lane_below(border, smoother.shape[0]), before[level][:, half], smoother)
                detail = approx - smoother
                score = score + gain_ref[level] * detail * detail
                approx = smoother
            yield at, score
        before = after


def state_of(score, colours):
    peak = jnp.max(score, axis=0).astype(jnp.bfloat16)
    weight = jnp.exp(score - peak.astype(jnp.float32)[None])
    total = jnp.sum(weight, axis=0)
    inverse = 1.0 / total
    means = [jnp.sum(weight * colour.astype(jnp.float32), axis=0) * inverse for colour in colours]
    return [peak, total.astype(jnp.bfloat16)] + [mean.astype(jnp.bfloat16) for mean in means]


def inner_kernel(
    gain_ref, planes_ref, taps_ref, lum_ref, row_ref, col_ref, state_ref, spread_ref, gain, inner, high, low, arrived
):
    depth, _, rows, columns = planes_ref.shape
    bands, _, share, _ = state_ref.shape
    count = rows - 2 * HALO
    tile, tiles = lax.axis_index("tile"), lax.axis_size("tile")
    tile_case = jnp.where(tile == 0, 0, jnp.where(tile == tiles - 1, 2, 1))
    lines, first = inner.shape[0], col_ref.shape[0]
    edge = pl.multiple_of(first + lines + tile_case * row_ref.shape[0], LANES)
    copies = []
    copies.append(pltpu.make_async_copy(gain_ref, gain, arrived.at[0]))
    copies[0].start()
    for start, target in ((first, inner), (0, col_ref), (edge, row_ref)):
        source = taps_ref.at[pl.ds(start, target.shape[0])]
        copies.append(pltpu.make_async_copy(source, target, arrived.at[len(copies)]))
        copies[-1].start()
    for plane in range(depth):
        lum_ref[plane] = luminance_of([planes_ref[plane, channel] for channel in range(3)])
    copies[1].wait()
    filter_rows(inner, rows, lambda plane, at: lum_ref[plane, :, at], depth, columns, high, low)
    copies[0].wait()
    for level in range(LEVELS):
        spread_ref[level] = jnp.full((1, LANES), gain[level], jnp.float32)
    copies[2].wait()
    inside = pl.ds(HALO, count)
    for at, score in scores(columns, lambda at: lum_ref[:, inside, at], gain, col_ref, high, low):
        colours = [planes_ref[:, channel, inside, at] for channel in range(3)]
        for k, part in enumerate(state_of(score.reshape(depth, count, LANES), colours)):
            state_ref[:, k, :, at] = part.reshape(bands, share, LANES)
    copies[3].wait()


def inner_state(planes, level_gain, groups, tiles):
    depth, channels, rows, columns = planes.shape
    count, share = rows - 2 * HALO, rows // groups
    taps = jnp.asarray(filters(columns, rows, tiles))
    inner_lines, edge_lines = 6 * count, 12 * HALO
    vmem = pl.BlockSpec(memory_space=pltpu.VMEM)
    window_lines = taps.shape[0] - inner_lines - 3 * edge_lines
    shapes = [(depth, rows, columns), (edge_lines, WINDOW), (window_lines, WINDOW), (count // share, 5, share, columns)]
    wide = len(windows_of(columns)) * WINDOW
    return pl.pallas_call(
        inner_kernel,
        out_shape=[jax.ShapeDtypeStruct(shape, jnp.bfloat16) for shape in shapes]
        + [jax.ShapeDtypeStruct((LEVELS, 1, LANES), jnp.float32)],
        in_specs=[pl.BlockSpec(memory_space=pl.ANY), vmem, pl.BlockSpec(memory_space=pl.ANY)],
        out_specs=[vmem] * (len(shapes) + 1),
        scratch_shapes=[
            pltpu.SMEM((LEVELS,), jnp.float32),
            pltpu.VMEM((inner_lines, WINDOW), jnp.bfloat16),
            pltpu.VMEM((LEVELS, depth * count, wide), jnp.bfloat16),
            pltpu.VMEM((LEVELS, depth * count, wide), jnp.bfloat16),
            pltpu.SemaphoreType.DMA((4,)),
        ],
        compiler_params=pltpu.CompilerParams(vmem_limit_bytes=43 * 2**20),
        cost_estimate=pl.CostEstimate(flops=2**30, bytes_accessed=10 * 2**20, transcendentals=0),
        name="inner_state",
    )(level_gain, planes, taps)


def edge_state_kernel(slow, planes_ref, lum_ref, row_ref, col_ref, inner_ref, gain_ref, core_ref, far_ref, *refs):
    *outs, halo, high, low, held = refs
    depth, _, rows, columns = planes_ref.shape
    groups, _, share, _ = held.shape
    fast = groups // slow
    split = outs[0].shape[-1]
    odd = lax.axis_index("tile") % 2

    def place_halo(above_ref, below_ref):
        halo[0] = above_ref[...]
        halo[1] = below_ref[...]

    pl.when(odd == 0)(lambda: place_halo(far_ref, core_ref))
    pl.when(odd == 1)(lambda: place_halo(core_ref, far_ref))

    def window_of(plane, at):
        return jnp.concatenate([halo[0, plane, :, at], lum_ref[plane, :, at], halo[1, plane, :, at]], axis=0)

    def edges_of(ref, *index):
        return jnp.concatenate([ref[index[:-1] + (pl.ds(start, HALO), index[-1])] for start in (0, rows - HALO)], axis=-2)

    filter_rows(row_ref, rows + 2 * HALO, window_of, depth, columns, high, low)
    side = HALO // share
    held[side : groups - side] = inner_ref[...]
    for at, score in scores(columns, lambda at: edges_of(lum_ref, slice(None), at), gain_ref, col_ref, high, low):
        colours = [edges_of(planes_ref, slice(None), channel, at) for channel in range(3)]
        for k, part in enumerate(state_of(score.reshape(depth, 2 * HALO, LANES), colours)):
            held[:side, k, :, at] = part[:HALO].reshape(side, share, LANES)
            held[groups - side :, k, :, at] = part[HALO:].reshape(side, share, LANES)

    group = lax.axis_index("gz")
    mine_slow, mine_fast = group // fast, group % fast
    for other in range(fast):
        for place in range(slow):
            outs[other][place] = held[place * fast + (mine_fast ^ other), :, :, :split]
    for other in range(slow):
        for place in range(fast):
            outs[fast + other][place] = held[(mine_slow ^ other) * fast + place, :, :, split:]


def edge_state(planes, inner, core, far, slow, groups, split):
    depth, _, rows, columns = planes.shape
    fast, share = groups // slow, rows // groups
    vmem = pl.BlockSpec(memory_space=pltpu.VMEM)
    wide = len(windows_of(columns)) * WINDOW
    shapes = [(slow, 5, share, split)] * fast + [(fast, 5, share, columns - split)] * slow
    return pl.pallas_call(
        functools.partial(edge_state_kernel, slow),
        out_shape=[jax.ShapeDtypeStruct(shape, jnp.bfloat16) for shape in shapes],
        in_specs=[vmem] * 8,
        out_specs=[vmem] * len(shapes),
        scratch_shapes=[
            pltpu.VMEM((2, depth, HALO, columns), jnp.bfloat16),
            pltpu.VMEM((LEVELS, 2 * depth * HALO, wide), jnp.bfloat16),
            pltpu.VMEM((LEVELS, 2 * depth * HALO, wide), jnp.bfloat16),
            pltpu.VMEM((groups, 5, share, columns), jnp.bfloat16),
        ],
        compiler_params=pltpu.CompilerParams(vmem_limit_bytes=40 * 2**20),
        name="edge_state",
    )(planes, *inner, core, far)


def merge_kernel(count, pick, *refs):
    states, outs, held = refs[:count], refs[count:-1], refs[-1]
    for place in range(held.shape[0]):
        for k, part in enumerate(combine([[state[place, k] for k in range(5)] for state in states])):
            held[place, k] = part.astype(jnp.bfloat16)
    place = pick(lax.axis_index("gz"))
    for other, out in enumerate(outs):
        out[...] = held[place ^ other]


def merge(states, pick):
    bands, _, share, columns = states[0].shape
    return pl.pallas_call(
        functools.partial(merge_kernel, len(states), pick),
        out_shape=[jax.ShapeDtypeStruct((5, share, columns), jnp.bfloat16)] * bands,
        scratch_shapes=[pltpu.VMEM(states[0].shape, jnp.bfloat16)],
        compiler_params=pltpu.CompilerParams(vmem_limit_bytes=16 * 2**20),
        name="merge",
    )(*states)


def join_kernel(counts, *refs):
    *refs, out_ref = refs
    start = 0
    for count in counts:
        states, refs = refs[:count], refs[count:]
        width = states[0].shape[-1]
        merged = combine([[state[k] for k in range(5)] for state in states])
        for channel in range(3):
            out_ref[channel, :, start : start + width] = merged[2 + channel].astype(jnp.bfloat16)
        start += width


def join(*parts):
    share = parts[0][0].shape[1]
    columns = sum(part[0].shape[2] for part in parts)
    return pl.pallas_call(
        functools.partial(join_kernel, [len(part) for part in parts]),
        out_shape=jax.ShapeDtypeStruct((3, share, columns), jnp.bfloat16),
        compiler_params=pltpu.CompilerParams(vmem_limit_bytes=16 * 2**20),
        name="join",
    )(*[state for part in parts for state in part])


def swap(states, groups, step, order):
    moved = [lax.ppermute(states[k], "gz", [(i, i ^ (k * step)) for i in range(groups)]) for k in order]
    return [states[0]] + moved


def per_device(planes, level_gain):
    columns = planes.shape[3]
    tiles = lax.axis_size("tile")
    groups = lax.axis_size("gz")
    slow = min(4, groups)
    fast = groups // slow
    split = 5 * columns // 8
    stack, to_core, to_far = fetch(planes)
    core = lax.ppermute(to_core, "tile", [(i, i ^ 1) for i in range(tiles)])
    between = range(1, tiles - 1, 2)
    far = lax.ppermute(to_far, "tile", [(i, i + 1) for i in between] + [(i + 1, i) for i in between])
    inner = inner_state(stack, level_gain, groups, tiles)
    states = edge_state(stack, inner, core, far, slow, groups, split)
    near = range(1, fast)
    first = swap(states[:fast], groups, 1, near)
    second = swap(states[fast:], groups, fast, FAR_FIRST)
    first = swap(merge(first, lambda group: group // fast), groups, fast, range(1, slow))
    second = swap(merge(second, lambda group: group % fast), groups, 1, near)
    return join(first, second)


def solution(mesh):
    return jax.shard_map(
        per_device,
        mesh=mesh,
        in_specs=(P("gz", None, "tile", None), P()),
        out_specs=P(None, ("tile", "gz"), None),
        check_vma=False,
    )
```
